32 devices in a mesh: head: 2 (over y), inner: 2 (over x), outer: 8 (over z, core).
Axes of the slice: x: 2, y: 2, z: 4, core: 2. Of those that a mesh axis runs over, the one named last changes fastest.
Arguments:
- query_nope: bfloat16 [2048, 8192], P(('inner', 'outer'), 'head'), may hold values from -6 to 6
- query_rope: bfloat16 [2048, 4096], P(('inner', 'outer'), 'head'), may hold values from -256 to 256
- latent: bfloat16 [2048, 512], P(('inner', 'outer')), may hold values from -6 to 6
- key_rope: bfloat16 [2048, 64], P(('inner', 'outer')), may hold values from -4 to 4
- key_up: bfloat16 [512, 8192], P(None, 'head'), may hold values from -0.25 to 0.25
- value_up: bfloat16 [512, 8192], P(None, 'head'), may hold values from -0.25 to 0.25
- latent_out: bfloat16 [2048, 32768], P(('inner', 'outer'), 'head'), may hold values from -3 to 3
- out_grad: bfloat16 [2048, 8192], P(('inner', 'outer'), 'head'), may hold values from -6 to 6
- logsum: float32 [2048, 64], P(('inner', 'outer'), 'head'), may hold values from 0 to 5000
- block_order: int32 [32], replicated, may hold values from 0 to 31, as said below
Outputs:
- d_query_nope: bfloat16 [2048, 8192], P(('inner', 'outer'), 'head')
- d_query_rope: bfloat16 [2048, 4096], P(('inner', 'outer'), 'head')
- d_latent: bfloat16 [2048, 512], P(('inner', 'outer'))
- d_key_rope: bfloat16 [2048, 64], P(('inner', 'outer'))
- d_key_up: float32 [512, 8192], P(('inner', 'outer'), 'head')
- d_value_up: float32 [512, 8192], P(('inner', 'outer'), 'head')
The draws below stay inside these ranges and needn't reach their ends.
Inputs may be any that keep to these rules, and one draw needn't show every extreme that they name: `block_order`: stored blocks 2 r and 2 r + 1 hold sequence blocks c and 31 - c for some c, in either order; every sequence block is held once.
All inputs are finite; a program needn't handle non-finite values.
Results may differ from the reference program's by a relative error of at most 0.0085.
The reference program's roundings to bfloat16 on the way count: a program that leaves them out, or rounds other values in their place, can miss the bound.
Values may be sent and summed in bfloat16 or wider, within the bound.
A program may use at most 128 MiB of HBM per device.

```python
import jax
import jax.numpy as jnp
from jax import lax

HEADS = 64
LATENT = 512
ROPE_DIM = 64
NOPE_DIM = 128
VALUE_DIM = 128
BLOCK_ROWS = 64
SEQUENCE = 2048
BLOCKS = 32


def rope_helper(key):
    baseline = jnp.clip(jax.random.normal(jax.random.fold_in(key, 11), (SEQUENCE, ROPE_DIM), jnp.float32), -4.0, 4.0)
    return baseline


def draw_key_rope(key, part):
    baseline = rope_helper(key)
    return baseline.astype(jnp.bfloat16)


def draw_query_rope(key, part):
    values = jnp.clip(jax.random.normal(jax.random.fold_in(key, 14), (SEQUENCE, HEADS * ROPE_DIM), jnp.float32), -4.0, 4.0)
    return values.astype(jnp.bfloat16)


def draw_block_order(key, part):
    pairs = BLOCKS // 2
    smaller = jax.random.permutation(jax.random.fold_in(key, 21), pairs).astype(jnp.int32)
    flipped = jax.random.randint(jax.random.fold_in(key, 22), (pairs,), 0, 2)
    larger = BLOCKS - 1 - smaller
    first_held = jnp.where(flipped == 1, larger, smaller)
    second_held = jnp.where(flipped == 1, smaller, larger)
    return jnp.stack([first_held, second_held], axis=1).reshape(BLOCKS).astype(jnp.int32)


def draw_logsum(key, part):
    order = draw_block_order(key, part)
    indices = jnp.arange(SEQUENCE, dtype=jnp.int32)
    places = (order[indices // BLOCK_ROWS] * BLOCK_ROWS + indices % BLOCK_ROWS).astype(jnp.float32)
    counted = jnp.log(places + 1.0) + 1.5
    noise = jax.random.uniform(jax.random.fold_in(key, 31), (SEQUENCE, HEADS), jnp.float32, 0.0, 1.0)
    values = counted[:, None] + noise
    return jnp.clip(values, 0.0, 5000.0).astype(jnp.float32)


def steps_of(own_key, shape, split, low, largest):
    def one(position, blocks):
        heights = jax.random.uniform(jax.random.fold_in(jax.random.fold_in(own_key, 6), position), (blocks,), jnp.float32, low / len(split), largest / len(split))
        return jnp.repeat(jnp.exp(heights), shape[position] // blocks).reshape((-1,) + (1,) * (len(shape) - position - 1))

    gain = one(*split[0])
    for cut in split[1:]:
        gain = gain * one(*cut)
    return gain


def centred(stream_key, dims, deviation, limit, split=(), kind=jnp.bfloat16):
    entries = deviation * jax.random.normal(stream_key, dims, jnp.float32)
    if split:
        entries = entries * steps_of(stream_key, dims, split, -0.22, 0.18)
    return jnp.clip(entries, -limit, limit).astype(kind)


def setup_inputs(seed: int = 0) -> dict:
    arg_keys = jax.random.split(jax.random.key(seed), 11)
    return {
        "query_nope": centred(arg_keys[0], (SEQUENCE, HEADS * NOPE_DIM), 1.0, 6.0, ((0, 16), (1, 2))),
        "query_rope": draw_query_rope(jax.random.fold_in(arg_keys[10], 71), 0),
        "latent": centred(arg_keys[2], (SEQUENCE, LATENT), 1.0, 6.0, ((0, 16),)),
        "key_rope": draw_key_rope(jax.random.fold_in(arg_keys[10], 71), 0),
        "key_up": centred(arg_keys[4], (LATENT, HEADS * NOPE_DIM), LATENT ** -0.5, 0.25, ((1, 2),)),
        "value_up": centred(arg_keys[5], (LATENT, HEADS * VALUE_DIM), LATENT ** -0.5, 0.25, ((1, 2),)),
        "latent_out": centred(arg_keys[6], (SEQUENCE, HEADS * LATENT), 0.5, 3.0, ((0, 16), (1, 2))),
        "out_grad": centred(arg_keys[7], (SEQUENCE, HEADS * VALUE_DIM), 1.0, 6.0, ((0, 16), (1, 2))),
        "logsum": draw_logsum(jax.random.fold_in(arg_keys[10], 71), 0),
        "block_order": draw_block_order(jax.random.fold_in(arg_keys[10], 71), 0),
    }


def stored_positions(block_order):
    indices = jnp.arange(SEQUENCE, dtype=jnp.int32)
    return block_order[indices // BLOCK_ROWS].astype(jnp.int32) * BLOCK_ROWS + indices % BLOCK_ROWS


def by_head(matrix, width):
    return matrix.reshape(matrix.shape[0], HEADS, width).transpose(1, 0, 2)


def from_heads(stacked):
    return stacked.transpose(1, 0, 2).reshape(stacked.shape[1], stacked.shape[0] * stacked.shape[2])


def reference(query_nope, query_rope, latent, key_rope, key_up, value_up, latent_out, out_grad, logsum, block_order):
    factor = float(NOPE_DIM + ROPE_DIM) ** -0.5
    positions = stored_positions(block_order)
    visible = positions[None, :] <= positions[:, None]

    def one_head(carried, inputs):
        nope_part, rope_part, saved, upstream, key_map, value_map, row_total = inputs
        query_latent = jnp.dot(nope_part, key_map.T, preferred_element_type=jnp.float32).astype(jnp.bfloat16)
        grad_latent = jnp.dot(upstream, value_map.T, preferred_element_type=jnp.float32).astype(jnp.bfloat16)
        scores = (jnp.dot(query_latent, latent.T, preferred_element_type=jnp.float32)
                  + jnp.dot(rope_part, key_rope.T, preferred_element_type=jnp.float32)) * factor
        probs = jnp.where(visible, jnp.exp(jnp.where(visible, scores - row_total, 0.0)), 0.0)
        dprobs = jnp.dot(grad_latent, latent.T, preferred_element_type=jnp.float32)
        row_delta = jnp.sum(grad_latent.astype(jnp.float32) * saved.astype(jnp.float32), axis=1, keepdims=True)
        dscore = (probs * (dprobs - row_delta) * factor).astype(jnp.bfloat16)
        probs_low = probs.astype(jnp.bfloat16)
        grad_query = jnp.dot(dscore, latent, preferred_element_type=jnp.float32).astype(jnp.bfloat16)
        grad_rope = jnp.dot(dscore, key_rope, preferred_element_type=jnp.float32).astype(jnp.bfloat16)
        grad_nope = jnp.dot(grad_query, key_map, preferred_element_type=jnp.float32).astype(jnp.bfloat16)
        latent_sum = (carried[0] + jnp.dot(dscore.T, query_latent, preferred_element_type=jnp.float32)
                      + jnp.dot(probs_low.T, grad_latent, preferred_element_type=jnp.float32))
        rope_sum = carried[1] + jnp.dot(dscore.T, rope_part, preferred_element_type=jnp.float32)
        key_grad = jnp.dot(grad_query.T, nope_part, preferred_element_type=jnp.float32)
        value_grad = jnp.dot(saved.T, upstream, preferred_element_type=jnp.float32)
        return (latent_sum, rope_sum), (grad_nope, grad_rope, key_grad, value_grad)

    start = (jnp.zeros((SEQUENCE, LATENT), jnp.float32), jnp.zeros((SEQUENCE, ROPE_DIM), jnp.float32))
    inputs = (by_head(query_nope, NOPE_DIM), by_head(query_rope, ROPE_DIM), by_head(latent_out, LATENT),
              by_head(out_grad, VALUE_DIM), by_head(key_up, NOPE_DIM), by_head(value_up, VALUE_DIM),
              by_head(logsum, 1))
    sums, stacked = lax.scan(one_head, start, inputs)
    return (from_heads(stacked[0]), from_heads(stacked[1]), sums[0].astype(jnp.bfloat16),
            sums[1].astype(jnp.bfloat16), from_heads(stacked[2]), from_heads(stacked[3]))
```

```python
import functools

import jax
import jax.numpy as jnp
from jax import lax
from jax.experimental import pallas as pl
from jax.experimental.pallas import tpu as pltpu
from jax.sharding import PartitionSpec as P

LATENT = 512
ROPE_DIM = 64
NOPE_DIM = 128
VALUE_DIM = 128
WIDE = 640
SPAN = 4
FACTOR = float(NOPE_DIM + ROPE_DIM) ** (-0.5)
VMEM = 60 * 1024 * 1024


def contract_last(first_op, second_op):
    return lax.dot_general(
        first_op, second_op, (((1,), (1,)), ((), ())), preferred_element_type=jnp.float32
    )


def contract_first(first_op, second_op):
    return lax.dot_general(
        first_op, second_op, (((0,), (0,)), ((), ())), preferred_element_type=jnp.float32
    )


def value_kernel(group, saved_ref, upstream_ref, out_ref):
    for h in range(group):
        saved = saved_ref[:, h * LATENT : (h + 1) * LATENT]
        upstream = upstream_ref[:, h * VALUE_DIM : (h + 1) * VALUE_DIM]
        out_ref[:, h * VALUE_DIM : (h + 1) * VALUE_DIM] = contract_first(saved, upstream).astype(
            out_ref.dtype
        )


def value_weights(latent_out, out_grad, group):
    tokens, width = out_grad.shape
    heads = width // VALUE_DIM
    return pl.pallas_call(
        functools.partial(value_kernel, group),
        grid=(heads // group,),
        in_specs=[
            pl.BlockSpec((tokens, group * LATENT), lambda i: (0, i)),
            pl.BlockSpec((tokens, group * VALUE_DIM), lambda i: (0, i)),
        ],
        out_specs=pl.BlockSpec((LATENT, group * VALUE_DIM), lambda i: (0, i)),
        out_shape=jax.ShapeDtypeStruct((LATENT, width), jnp.bfloat16),
        compiler_params=pltpu.CompilerParams(vmem_limit_bytes=VMEM),
        name="value_weights",
    )(latent_out, out_grad)


def attention_kernel(
    group,
    block,
    blocks,
    places_ref,
    nope_ref,
    rope_ref,
    lat_ref,
    key_rope_ref,
    key_up_ref,
    value_up_ref,
    saved_ref,
    upstream_ref,
    logsum_ref,
    d_nope_ref,
    d_rope_ref,
    d_keys_ref,
    key_weight_ref,
    keys,
    key_sums,
    queries,
    grads,
    delta,
    query_sums,
):
    rows = group * block
    tile = SPAN * block
    step = pl.program_id(0)

    @pl.when(step == 0)
    def _():
        def sort(p, carry):
            src = pl.ds(pl.multiple_of(places_ref[2 + p] * block, block), block)
            dst = pl.ds(pl.multiple_of(p * block, block), block)
            keys[dst, :LATENT] = lat_ref[src, :]
            part = key_rope_ref[src, :]
            keys[dst, LATENT:] = jnp.concatenate([part, jnp.zeros_like(part)], axis=1)
            return carry

        lax.fori_loop(0, blocks, sort, 0)
        key_sums[...] = jnp.zeros_like(key_sums)

    query_sums[...] = jnp.zeros_like(query_sums)
    for h in range(group):
        nope = nope_ref[:, h * NOPE_DIM : (h + 1) * NOPE_DIM]
        key_map = key_up_ref[:, h * NOPE_DIM : (h + 1) * NOPE_DIM]
        lat = contract_last(nope, key_map).astype(jnp.bfloat16)
        upstream = upstream_ref[:, h * VALUE_DIM : (h + 1) * VALUE_DIM]
        value_map = value_up_ref[:, h * VALUE_DIM : (h + 1) * VALUE_DIM]
        grad = contract_last(upstream, value_map).astype(jnp.bfloat16)
        for t in range(2):
            mine = slice(h * block, (h + 1) * block)
            held = slice(t * block, (t + 1) * block)
            queries[t, mine, :LATENT] = lat[held]
            part = rope_ref[held, h * ROPE_DIM : (h + 1) * ROPE_DIM]
            queries[t, mine, LATENT:] = jnp.concatenate([part, jnp.zeros_like(part)], axis=1)
            grads[t, mine, :] = grad[held]
    for t in range(2):
        held = slice(t * block, (t + 1) * block)
        for h in range(0, group, 2):
            saved = jnp.concatenate(
                [saved_ref[held, k * LATENT : (k + 1) * LATENT] for k in (h, h + 1)], axis=0
            )
            mine = slice(h * block, (h + 2) * block)
            product = grads[t, mine, :].astype(jnp.float32) * saved.astype(jnp.float32)
            folded = product[:, :128]
            for k in range(128, LATENT, 128):
                folded = folded + product[:, k : k + 128]
            delta[t, :, mine] = jnp.sum(folded.T, axis=0, keepdims=True)

    split = places_ref[0] // SPAN + 1
    key_index = lax.broadcasted_iota(jnp.int32, (tile, rows), 0)
    row_index = lax.rem(lax.broadcasted_iota(jnp.int32, (tile, rows), 1), block)
    apart = key_index - row_index

    def visit(i, carry):
        second = (i >= split).astype(jnp.int32)
        index = i - second * split
        place = places_ref[second]
        near = pl.ds(pl.multiple_of(index * tile, tile), tile)
        query = queries[second]
        grad = grads[second]
        held = keys[near, :]
        scores = contract_last(held, query) * FACTOR
        visible = apart <= place * block - index * tile
        weights = jnp.where(visible, jnp.exp(scores - logsum_ref[second]), 0.0)
        dprobs = contract_last(held[:, :LATENT], grad)
        dscore = (weights * (dprobs - delta[second]) * FACTOR).astype(jnp.bfloat16)
        rounded = weights.astype(jnp.bfloat16)
        query_sums[second] += contract_first(dscore, held)
        from_scores = jnp.dot(dscore, query, preferred_element_type=jnp.float32)
        from_values = jnp.dot(rounded, grad, preferred_element_type=jnp.float32)
        key_sums[near, :LATENT] += from_scores[:, :LATENT] + from_values
        key_sums[near, LATENT:] += from_scores[:, LATENT:]
        return carry

    lax.fori_loop(0, blocks // SPAN + 1, visit, 0)

    for h in range(group):
        mine = slice(h * block, (h + 1) * block)
        cols = slice(h * NOPE_DIM, (h + 1) * NOPE_DIM)
        grad_query = jnp.concatenate([query_sums[t, mine, :LATENT] for t in range(2)], axis=0)
        grad_query = grad_query.astype(jnp.bfloat16)
        key_map = key_up_ref[:, cols]
        d_nope_ref[:, cols] = jnp.dot(
            grad_query, key_map, preferred_element_type=jnp.float32
        ).astype(jnp.bfloat16)
        key_weight_ref[:, cols] = contract_first(grad_query, nope_ref[:, cols]).astype(
            key_weight_ref.dtype
        )
    for t in range(2):
        held = slice(t * block, (t + 1) * block)
        for h in range(0, group, 2):
            pair = [
                query_sums[t, k * block : (k + 1) * block, LATENT : LATENT + ROPE_DIM]
                for k in (h, h + 1)
            ]
            d_rope_ref[held, h * ROPE_DIM : (h + 2) * ROPE_DIM] = jnp.concatenate(
                pair, axis=1
            ).astype(jnp.bfloat16)

    @pl.when(step == pl.num_programs(0) - 1)
    def _():
        def restore(p, carry):
            dst = pl.ds(pl.multiple_of(places_ref[2 + p] * block, block), block)
            src = pl.ds(pl.multiple_of(p * block, block), block)
            d_keys_ref[dst, :] = key_sums[src, :].astype(d_keys_ref.dtype)
            return carry

        lax.fori_loop(0, blocks, restore, 0)


def attention(
    places, query_nope, query_rope, keys, key_rope, key_up, value_up, saved, upstream, logsum, group
):
    tokens = query_nope.shape[0]
    heads = query_nope.shape[1] // NOPE_DIM
    block = tokens // 2
    length = keys.shape[0]
    blocks = length // block
    rows = group * block
    totals = logsum.reshape(2, block, heads).transpose(0, 2, 1).reshape(2, 1, heads * block)
    whole = lambda i, places: (0, 0)
    part = lambda i, places: (0, i)
    pairs = length * heads * tokens // 2
    return pl.pallas_call(
        functools.partial(attention_kernel, group, block, blocks),
        grid_spec=pltpu.PrefetchScalarGridSpec(
            num_scalar_prefetch=1,
            grid=(heads // group,),
            in_specs=[
                pl.BlockSpec((tokens, group * NOPE_DIM), part),
                pl.BlockSpec((tokens, group * ROPE_DIM), part),
                pl.BlockSpec((length, LATENT), whole),
                pl.BlockSpec((length, ROPE_DIM), whole),
                pl.BlockSpec((LATENT, group * NOPE_DIM), part),
                pl.BlockSpec((LATENT, group * VALUE_DIM), part),
                pl.BlockSpec((tokens, group * LATENT), part),
                pl.BlockSpec((tokens, group * VALUE_DIM), part),
                pl.BlockSpec((2, 1, rows), lambda i, places: (0, 0, i)),
            ],
            out_specs=[
                pl.BlockSpec((tokens, group * NOPE_DIM), part),
                pl.BlockSpec((tokens, group * ROPE_DIM), part),
                pl.BlockSpec((length, WIDE), whole),
                pl.BlockSpec((LATENT, group * NOPE_DIM), part),
            ],
            scratch_shapes=[
                pltpu.VMEM((length, WIDE), jnp.bfloat16),
                pltpu.VMEM((length, WIDE), jnp.float32),
                pltpu.VMEM((2, rows, WIDE), jnp.bfloat16),
                pltpu.VMEM((2, rows, LATENT), jnp.bfloat16),
                pltpu.VMEM((2, 1, rows), jnp.float32),
                pltpu.VMEM((2, rows, WIDE), jnp.float32),
            ],
        ),
        out_shape=[
            jax.ShapeDtypeStruct(query_nope.shape, jnp.bfloat16),
            jax.ShapeDtypeStruct(query_rope.shape, jnp.bfloat16),
            jax.ShapeDtypeStruct((length, WIDE), jnp.bfloat16),
            jax.ShapeDtypeStruct((LATENT, heads * NOPE_DIM), jnp.bfloat16),
        ],
        compiler_params=pltpu.CompilerParams(vmem_limit_bytes=VMEM),
        cost_estimate=pl.CostEstimate(
            flops=pairs * 2 * 2752, bytes_accessed=20 * 1024 * 1024, transcendentals=pairs
        ),
        name="attention",
    )(places, query_nope, query_rope, keys, key_rope, key_up, value_up, saved, upstream, totals)


def local(
    query_nope,
    query_rope,
    latent,
    key_rope,
    key_up,
    value_up,
    latent_out,
    out_grad,
    logsum,
    block_order,
):
    axes = ("inner", "outer")
    heads = query_nope.shape[1] // NOPE_DIM
    blocks = block_order.shape[0]
    group = min(8, heads)
    all_keys = lax.all_gather(latent, axes, axis=0, tiled=True)
    all_rope = lax.all_gather(key_rope, axes, axis=0, tiled=True)
    index = lax.iota(jnp.int32, blocks)
    held = (block_order[:, None] == index[None, :]).astype(jnp.int32)
    stored = jnp.sum(held * index[:, None], axis=0)
    first = 2 * lax.axis_index(axes)
    own = lax.dynamic_slice_in_dim(block_order, first, 2, 0)
    places = jnp.concatenate([own, stored])
    value_weight = value_weights(latent_out, out_grad, group)
    d_value_up = lax.psum_scatter(value_weight, axes, scatter_dimension=0, tiled=True)
    d_nope, d_rope, d_keys, key_weight = attention(
        places,
        query_nope,
        query_rope,
        all_keys,
        all_rope,
        key_up,
        value_up,
        latent_out,
        out_grad,
        logsum,
        group,
    )
    own_keys = lax.psum_scatter(d_keys, axes, scatter_dimension=0, tiled=True)
    own_keys = lax.psum(own_keys, "head")
    d_key_up = lax.psum_scatter(key_weight, axes, scatter_dimension=0, tiled=True)
    return (
        d_nope,
        d_rope,
        own_keys[:, :LATENT],
        own_keys[:, LATENT : LATENT + ROPE_DIM],
        d_key_up.astype(jnp.float32),
        d_value_up.astype(jnp.float32),
    )


def solution(mesh):
    placed = (
        P(("inner", "outer"), "head"),
        P(("inner", "outer"), "head"),
        P(("inner", "outer"), None),
        P(("inner", "outer"), None),
        P(None, "head"),
        P(None, "head"),
        P(("inner", "outer"), "head"),
        P(("inner", "outer"), "head"),
        P(("inner", "outer"), "head"),
        P(),
    )
    return jax.shard_map(
        local,
        mesh=mesh,
        in_specs=placed,
        out_specs=(
            P(("inner", "outer"), "head"),
            P(("inner", "outer"), "head"),
            P(("inner", "outer"), None),
            P(("inner", "outer"), None),
            P(("inner", "outer"), "head"),
            P(("inner", "outer"), "head"),
        ),
        check_vma=False,
    )
```

```python
import functools

import jax
import jax.numpy as jnp
from jax import lax
from jax.experimental import pallas as pl
from jax.experimental.pallas import tpu as pltpu
from jax.sharding import PartitionSpec as P

LATENT = 512
ROPE_DIM = 64
NOPE_DIM = 128
VALUE_DIM = 128
WIDE = 640
SPAN = 4
FACTOR = float(NOPE_DIM + ROPE_DIM) ** (-0.5)
VMEM = 60 * 1024 * 1024


def contract_last(first_op, second_op):
    return lax.dot_general(
        first_op, second_op, (((1,), (1,)), ((), ())), preferred_element_type=jnp.float32
    )


def contract_first(first_op, second_op):
    return lax.dot_general(
        first_op, second_op, (((0,), (0,)), ((), ())), preferred_element_type=jnp.float32
    )


def value_kernel(group, saved_ref, upstream_ref, out_ref):
    for h in range(group):
        saved = saved_ref[:, h * LATENT : (h + 1) * LATENT]
        upstream = upstream_ref[:, h * VALUE_DIM : (h + 1) * VALUE_DIM]
        out_ref[:, h * VALUE_DIM : (h + 1) * VALUE_DIM] = contract_first(saved, upstream).astype(
            out_ref.dtype
        )


def value_weights(latent_out, out_grad, group):
    tokens, width = out_grad.shape
    heads = width // VALUE_DIM
    return pl.pallas_call(
        functools.partial(value_kernel, group),
        grid=(heads // group,),
        in_specs=[
            pl.BlockSpec((tokens, group * LATENT), lambda i: (0, i)),
            pl.BlockSpec((tokens, group * VALUE_DIM), lambda i: (0, i)),
        ],
        out_specs=pl.BlockSpec((LATENT, group * VALUE_DIM), lambda i: (0, i)),
        out_shape=jax.ShapeDtypeStruct((LATENT, width), jnp.bfloat16),
        compiler_params=pltpu.CompilerParams(vmem_limit_bytes=VMEM),
        name="value_weights",
    )(latent_out, out_grad)


def attention_kernel(
    group,
    block,
    blocks,
    places_ref,
    nope_ref,
    rope_ref,
    lat_ref,
    key_up_ref,
    value_up_ref,
    saved_ref,
    upstream_ref,
    logsum_ref,
    d_nope_ref,
    d_rope_ref,
    d_keys_ref,
    key_weight_ref,
    keys,
    key_sums,
    queries,
    grads,
    delta,
    query_sums,
):
    rows = group * block
    tile = SPAN * block
    step = pl.program_id(0)

    @pl.when(step == 0)
    def _():
        def sort(p, carry):
            src = pl.ds(pl.multiple_of(places_ref[2 + p] * block, block), block)
            dst = pl.ds(pl.multiple_of(p * block, block), block)
            keys[dst, :] = lat_ref[src, :]
            return carry

        lax.fori_loop(0, blocks, sort, 0)
        key_sums[...] = jnp.zeros_like(key_sums)

    query_sums[...] = jnp.zeros_like(query_sums)
    for h in range(group):
        nope = nope_ref[:, h * NOPE_DIM : (h + 1) * NOPE_DIM]
        key_map = key_up_ref[:, h * NOPE_DIM : (h + 1) * NOPE_DIM]
        lat = contract_last(nope, key_map).astype(jnp.bfloat16)
        upstream = upstream_ref[:, h * VALUE_DIM : (h + 1) * VALUE_DIM]
        value_map = value_up_ref[:, h * VALUE_DIM : (h + 1) * VALUE_DIM]
        grad = contract_last(upstream, value_map).astype(jnp.bfloat16)
        for t in range(2):
            mine = slice(h * block, (h + 1) * block)
            held = slice(t * block, (t + 1) * block)
            queries[t, mine, :LATENT] = lat[held]
            part = rope_ref[held, h * ROPE_DIM : (h + 1) * ROPE_DIM]
            queries[t, mine, LATENT:] = jnp.concatenate([part, jnp.zeros_like(part)], axis=1)
            grads[t, mine, :] = grad[held]
    for t in range(2):
        held = slice(t * block, (t + 1) * block)
        for h in range(0, group, 2):
            saved = jnp.concatenate(
                [saved_ref[held, k * LATENT : (k + 1) * LATENT] for k in (h, h + 1)], axis=0
            )
            mine = slice(h * block, (h + 2) * block)
            product = grads[t, mine, :].astype(jnp.float32) * saved.astype(jnp.float32)
            folded = product[:, :128]
            for k in range(128, LATENT, 128):
                folded = folded + product[:, k : k + 128]
            delta[t, :, mine] = jnp.sum(folded.T, axis=0, keepdims=True)

    split = places_ref[0] // SPAN + 1
    key_index = lax.broadcasted_iota(jnp.int32, (tile, rows), 0)
    row_index = lax.rem(lax.broadcasted_iota(jnp.int32, (tile, rows), 1), block)
    apart = key_index - row_index

    def visit(i, carry):
        second = (i >= split).astype(jnp.int32)
        index = i - second * split
        place = places_ref[second]
        near = pl.ds(pl.multiple_of(index * tile, tile), tile)
        query = queries[second]
        grad = grads[second]
        held = keys[near, :]
        scores = contract_last(held, query) * FACTOR
        visible = apart <= place * block - index * tile
        weights = jnp.where(visible, jnp.exp(scores - logsum_ref[second]), 0.0)
        dprobs = contract_last(held[:, :LATENT], grad)
        dscore = (weights * (dprobs - delta[second]) * FACTOR).astype(jnp.bfloat16)
        rounded = weights.astype(jnp.bfloat16)
        query_sums[second] += contract_first(dscore, held)
        from_scores = jnp.dot(dscore, query, preferred_element_type=jnp.float32)
        from_values = jnp.dot(rounded, grad, preferred_element_type=jnp.float32)
        key_sums[near, :LATENT] += from_scores[:, :LATENT] + from_values
        key_sums[near, LATENT:] += from_scores[:, LATENT:]
        return carry

    lax.fori_loop(0, blocks // SPAN + 1, visit, 0)

    for h in range(group):
        mine = slice(h * block, (h + 1) * block)
        cols = slice(h * NOPE_DIM, (h + 1) * NOPE_DIM)
        grad_query = jnp.concatenate([query_sums[t, mine, :LATENT] for t in range(2)], axis=0)
        grad_query = grad_query.astype(jnp.bfloat16)
        key_map = key_up_ref[:, cols]
        d_nope_ref[:, cols] = jnp.dot(
            grad_query, key_map, preferred_element_type=jnp.float32
        ).astype(jnp.bfloat16)
        key_weight_ref[:, cols] = contract_first(grad_query, nope_ref[:, cols]).astype(
            key_weight_ref.dtype
        )
    for t in range(2):
        held = slice(t * block, (t + 1) * block)
        for h in range(0, group, 2):
            pair = [
                query_sums[t, k * block : (k + 1) * block, LATENT : LATENT + ROPE_DIM]
                for k in (h, h + 1)
            ]
            d_rope_ref[held, h * ROPE_DIM : (h + 2) * ROPE_DIM] = jnp.concatenate(
                pair, axis=1
            ).astype(jnp.bfloat16)

    @pl.when(step == pl.num_programs(0) - 1)
    def _():
        def restore(p, carry):
            dst = pl.ds(pl.multiple_of(places_ref[2 + p] * block, block), block)
            src = pl.ds(pl.multiple_of(p * block, block), block)
            d_keys_ref[dst, :] = key_sums[src, :].astype(d_keys_ref.dtype)
            return carry

        lax.fori_loop(0, blocks, restore, 0)


def attention(
    places, query_nope, query_rope, keys, key_up, value_up, saved, upstream, logsum, group
):
    tokens = query_nope.shape[0]
    heads = query_nope.shape[1] // NOPE_DIM
    block = tokens // 2
    length = keys.shape[0]
    blocks = length // block
    rows = group * block
    totals = logsum.reshape(2, block, heads).transpose(0, 2, 1).reshape(2, 1, heads * block)
    whole = lambda i, places: (0, 0)
    part = lambda i, places: (0, i)
    pairs = length * heads * tokens // 2
    return pl.pallas_call(
        functools.partial(attention_kernel, group, block, blocks),
        grid_spec=pltpu.PrefetchScalarGridSpec(
            num_scalar_prefetch=1,
            grid=(heads // group,),
            in_specs=[
                pl.BlockSpec((tokens, group * NOPE_DIM), part),
                pl.BlockSpec((tokens, group * ROPE_DIM), part),
                pl.BlockSpec((length, WIDE), whole),
                pl.BlockSpec((LATENT, group * NOPE_DIM), part),
                pl.BlockSpec((LATENT, group * VALUE_DIM), part),
                pl.BlockSpec((tokens, group * LATENT), part),
                pl.BlockSpec((tokens, group * VALUE_DIM), part),
                pl.BlockSpec((2, 1, rows), lambda i, places: (0, 0, i)),
            ],
            out_specs=[
                pl.BlockSpec((tokens, group * NOPE_DIM), part),
                pl.BlockSpec((tokens, group * ROPE_DIM), part),
                pl.BlockSpec((length, WIDE), whole),
                pl.BlockSpec((LATENT, group * NOPE_DIM), part),
            ],
            scratch_shapes=[
                pltpu.VMEM((length, WIDE), jnp.bfloat16),
                pltpu.VMEM((length, WIDE), jnp.float32),
                pltpu.VMEM((2, rows, WIDE), jnp.bfloat16),
                pltpu.VMEM((2, rows, LATENT), jnp.bfloat16),
                pltpu.VMEM((2, 1, rows), jnp.float32),
                pltpu.VMEM((2, rows, WIDE), jnp.float32),
            ],
        ),
        out_shape=[
            jax.ShapeDtypeStruct(query_nope.shape, jnp.bfloat16),
            jax.ShapeDtypeStruct(query_rope.shape, jnp.bfloat16),
            jax.ShapeDtypeStruct((length, WIDE), jnp.bfloat16),
            jax.ShapeDtypeStruct((LATENT, heads * NOPE_DIM), jnp.bfloat16),
        ],
        compiler_params=pltpu.CompilerParams(vmem_limit_bytes=VMEM),
        cost_estimate=pl.CostEstimate(
            flops=pairs * 2 * 2752, bytes_accessed=20 * 1024 * 1024, transcendentals=pairs
        ),
        name="attention",
    )(places, query_nope, query_rope, keys, key_up, value_up, saved, upstream, totals)


MESH = pl.DeviceIdType.MESH


def device_at(place, axis, value):
    head, inner, outer = place
    if axis == "head":
        return (value, inner, outer)
    if axis == "inner":
        return (head, value, outer)
    if axis == "depth":
        return (head, inner, value * 2 + lax.rem(outer, 2))
    return (head, inner, outer - lax.rem(outer, 2) + value)


def where_am_i():
    head, inner, outer = (lax.axis_index(a) for a in ("head", "inner", "outer"))
    spot = {"head": head, "inner": inner, "depth": outer // 2, "core": lax.rem(outer, 2)}
    return (head, inner, outer), spot


def greet(place, spot, sizes, axes):
    barrier = pltpu.get_barrier_semaphore()
    count = 0
    for axis in axes:
        for k in range(1, sizes[axis]):
            target = lax.rem(spot[axis] + k, sizes[axis])
            pl.semaphore_signal(
                barrier, inc=1, device_id=device_at(place, axis, target), device_id_type=MESH
            )
            count += 1
    pl.semaphore_wait(barrier, count)


def gather_kernel(sizes, own_ref, out_ref, *sems):
    deep_send, deep_recv, side_send, side_recv, core_send, core_recv = sems
    place, spot = where_am_i()
    depth, sides = sizes["depth"], sizes["inner"]
    greet(place, spot, sizes, ("core", "depth", "inner"))
    inner, level, core = spot["inner"], spot["depth"], spot["core"]
    out_ref[inner, level, core] = own_ref[...]
    started = []

    def send(slot, axis, target, send_sem, recv_sem):
        copy = pltpu.make_async_remote_copy(
            src_ref=out_ref.at[slot],
            dst_ref=out_ref.at[slot],
            send_sem=send_sem,
            recv_sem=recv_sem,
            device_id=device_at(place, axis, target),
            device_id_type=MESH,
        )
        copy.start()
        started.append(copy)
        return copy

    def to_core(k, j):
        slot = (lax.rem(inner + sides - k, sides), lax.rem(level + depth - j, depth), core)
        return send(slot, "core", 1 - core, core_send.at[k, j], core_recv.at[k, j])

    def to_sides(j):
        slot = (inner, lax.rem(level + depth - j, depth), core)
        return [
            send(
                slot,
                "inner",
                lax.rem(inner + k, sides),
                side_send.at[k - 1, j],
                side_recv.at[k - 1, j],
            )
            for k in range(1, sides)
        ]

    deep = [
        send(
            (inner, level, core),
            "depth",
            lax.rem(level + k, depth),
            deep_send.at[k - 1],
            deep_recv.at[k - 1],
        )
        for k in range(1, depth)
    ]
    side = [to_sides(0)]
    last = [to_core(0, 0)]
    for j in range(1, depth):
        deep[j - 1].wait_recv()
        side.append(to_sides(j))
        last.append(to_core(0, j))
    for j in range(depth):
        for k in range(1, sides):
            side[j][k - 1].wait_recv()
            last.append(to_core(k, j))
    for copy in last:
        copy.wait_recv()
    for copy in started:
        copy.wait_send()


def gather_rows(own, sizes):
    depth, sides = sizes["depth"], sizes["inner"]
    dma = pltpu.SemaphoreType.DMA
    return pl.pallas_call(
        functools.partial(gather_kernel, sizes),
        in_specs=[pl.BlockSpec(memory_space=pltpu.VMEM)],
        out_specs=pl.BlockSpec(memory_space=pltpu.VMEM),
        out_shape=jax.ShapeDtypeStruct((sides, depth, 2) + own.shape, own.dtype),
        scratch_shapes=[
            dma((depth - 1,)),
            dma((depth - 1,)),
            dma((sides - 1, depth)),
            dma((sides - 1, depth)),
            dma((sides, depth)),
            dma((sides, depth)),
        ],
        compiler_params=pltpu.CompilerParams(
            collective_id=0, has_side_effects=True, vmem_limit_bytes=VMEM
        ),
        name="gather_keys",
    )(own)


def wide(x):
    return x.astype(jnp.float32)


def reduce_kernel(
    sizes,
    pieces,
    weight_ref,
    keys_ref,
    out_weight_ref,
    out_keys_ref,
    w_recv1,
    w_sum1,
    w_recv2,
    w_sum2,
    w_recv3,
    k_recv1,
    k_sum1,
    k_recv2,
    k_sum2,
    k_recv3,
    k_sum3,
    k_recv4,
    w1_send,
    w1_recv,
    w2_send,
    w2_recv,
    w3_send,
    w3_recv,
    k1_send,
    k1_recv,
    k2_send,
    k2_recv,
    k3_send,
    k3_recv,
    k4_send,
    k4_recv,
    k5_send,
    k5_recv,
):
    place, spot = where_am_i()
    depth, sides, heads = sizes["depth"], sizes["inner"], sizes["head"]
    greet(place, spot, sizes, ("core", "depth", "inner", "head"))
    inner, level, core, head = (spot[a] for a in ("inner", "depth", "core", "head"))
    width = weight_ref.shape[-1] // pieces
    share = keys_ref.shape[-2] // heads
    started = []

    def send(src, dst, axis, target, send_sem, recv_sem):
        copy = pltpu.make_async_remote_copy(
            src_ref=src,
            dst_ref=dst,
            send_sem=send_sem,
            recv_sem=recv_sem,
            device_id=device_at(place, axis, target),
            device_id_type=MESH,
        )
        copy.start()
        started.append(copy)
        return copy

    def scatter(axis, source, target_buffer, sends, recvs):
        out = []
        for k in range(1, sizes[axis]):
            target = lax.rem(spot[axis] + k, sizes[axis])
            out.append(
                send(
                    source(target), target_buffer(k - 1), axis, target, sends(k - 1), recvs(k - 1)
                )
            )
        return out

    def arrive(copies):
        for copy in copies:
            copy.wait_recv()

    keys_copy = send(keys_ref.at[:, :, 1 - core], k_recv1, "core", 1 - core, k1_send, k1_recv)
    cols = [slice(c * width, (c + 1) * width) for c in range(pieces)]
    first = [
        send(
            weight_ref.at[:, :, 1 - core, :, cols[c]],
            w_recv1.at[c],
            "core",
            1 - core,
            w1_send.at[c],
            w1_recv.at[c],
        )
        for c in range(pieces)
    ]
    keys_copy.wait_recv()
    for i in range(sides):
        for j in range(depth):
            k_sum1[i, j] = (wide(keys_ref[i, j, core]) + wide(k_recv1[i, j])).astype(k_sum1.dtype)

    def rows_of(target):
        return pl.ds(pl.multiple_of(target * share, share), share)

    k_heads = scatter(
        "head",
        lambda p: k_sum1.at[:, :, rows_of(p), :],
        lambda k: k_recv2.at[k],
        lambda k: k2_send.at[k],
        lambda k: k2_recv.at[k],
    )
    second = []
    for c in range(pieces):
        first[c].wait_recv()
        for i in range(sides):
            for j in range(depth):
                w_sum1[c, i, j] = (
                    wide(weight_ref[i, j, core, :, cols[c]]) + wide(w_recv1[c, i, j])
                ).astype(w_sum1.dtype)
        second.append(
            scatter(
                "inner",
                lambda p: w_sum1.at[c, p],
                lambda k: w_recv2.at[c, k],
                lambda k: w2_send.at[c, k],
                lambda k: w2_recv.at[c, k],
            )
        )
    arrive(k_heads)
    for i in range(sides):
        for j in range(depth):
            total = wide(k_sum1[i, j, rows_of(head), :])
            for k in range(heads - 1):
                total = total + wide(k_recv2[k, i, j])
            k_sum2[i, j] = total.astype(k_sum2.dtype)
    k_sides = scatter(
        "inner",
        lambda p: k_sum2.at[p],
        lambda k: k_recv3.at[k],
        lambda k: k3_send.at[k],
        lambda k: k3_recv.at[k],
    )
    third = []

    def middle(c):
        arrive(second[c])
        for j in range(depth):
            total = wide(w_sum1[c, inner, j])
            for k in range(sides - 1):
                total = total + wide(w_recv2[c, k, j])
            w_sum2[c, j] = total.astype(w_sum2.dtype)
        third.append(
            scatter(
                "depth",
                lambda p: w_sum2.at[c, p],
                lambda k: w_recv3.at[c, k],
                lambda k: w3_send.at[c, k],
                lambda k: w3_recv.at[c, k],
            )
        )

    for c in range(pieces - 1):
        middle(c)
    arrive(k_sides)
    for j in range(depth):
        total = wide(k_sum2[inner, j])
        for k in range(sides - 1):
            total = total + wide(k_recv3[k, j])
        k_sum3[j] = total.astype(k_sum3.dtype)
    k_depth = scatter(
        "depth",
        lambda p: k_sum3.at[p],
        lambda k: k_recv4.at[k],
        lambda k: k4_send.at[k],
        lambda k: k4_recv.at[k],
    )
    middle(pieces - 1)
    arrive(k_depth)
    total = wide(k_sum3[level])
    for k in range(depth - 1):
        total = total + wide(k_recv4[k])
    out_keys_ref[rows_of(head), :] = total.astype(out_keys_ref.dtype)
    k_last = [
        send(
            out_keys_ref.at[rows_of(head), :],
            out_keys_ref.at[rows_of(head), :],
            "head",
            lax.rem(head + k, heads),
            k5_send.at[k - 1],
            k5_recv.at[k - 1],
        )
        for k in range(1, heads)
    ]
    for c in range(pieces):
        arrive(third[c])
        total = wide(w_sum2[c, level])
        for k in range(depth - 1):
            total = total + wide(w_recv3[c, k])
        out_weight_ref[:, cols[c]] = total
    arrive(k_last)
    for copy in started:
        copy.wait_send()


def reduce_rows(weight, keys, sizes, pieces):
    depth, sides, heads = sizes["depth"], sizes["inner"], sizes["head"]
    owners = sides * depth * 2
    rows, width = weight.shape[0] // owners, weight.shape[1]
    tokens = keys.shape[0] // owners
    weight = weight.reshape(sides, depth, 2, rows, width)
    keys = keys.reshape(sides, depth, 2, tokens, keys.shape[1])
    piece = (rows, width // pieces)
    whole = (tokens, WIDE)
    part = (tokens // heads, WIDE)
    vmem = lambda *shape: pltpu.VMEM(shape, jnp.bfloat16)
    dma = pltpu.SemaphoreType.DMA
    return pl.pallas_call(
        functools.partial(reduce_kernel, sizes, pieces),
        in_specs=[pl.BlockSpec(memory_space=pltpu.VMEM)] * 2,
        out_specs=[pl.BlockSpec(memory_space=pltpu.VMEM)] * 2,
        out_shape=[
            jax.ShapeDtypeStruct((rows, width), jnp.float32),
            jax.ShapeDtypeStruct(whole, jnp.bfloat16),
        ],
        scratch_shapes=[
            vmem(pieces, sides, depth, *piece),
            vmem(pieces, sides, depth, *piece),
            vmem(pieces, sides - 1, depth, *piece),
            vmem(pieces, depth, *piece),
            vmem(pieces, depth - 1, *piece),
            vmem(sides, depth, *whole),
            vmem(sides, depth, *whole),
            vmem(heads - 1, sides, depth, *part),
            vmem(sides, depth, *part),
            vmem(sides - 1, depth, *part),
            vmem(depth, *part),
            vmem(depth - 1, *part),
            dma((pieces,)),
            dma((pieces,)),
            dma((pieces, sides - 1)),
            dma((pieces, sides - 1)),
            dma((pieces, depth - 1)),
            dma((pieces, depth - 1)),
            dma(()),
            dma(()),
            dma((heads - 1,)),
            dma((heads - 1,)),
            dma((sides - 1,)),
            dma((sides - 1,)),
            dma((depth - 1,)),
            dma((depth - 1,)),
            dma((heads - 1,)),
            dma((heads - 1,)),
        ],
        compiler_params=pltpu.CompilerParams(
            collective_id=1, has_side_effects=True, vmem_limit_bytes=VMEM
        ),
        name="reduce_gradients",
    )(weight, keys)


def local(
    query_nope,
    query_rope,
    latent,
    key_rope,
    key_up,
    value_up,
    latent_out,
    out_grad,
    logsum,
    block_order,
):
    axes = ("inner", "outer")
    heads = query_nope.shape[1] // NOPE_DIM
    blocks = block_order.shape[0]
    group = min(8, heads)
    sizes = {
        "head": lax.axis_size("head"),
        "inner": lax.axis_size("inner"),
        "depth": lax.axis_size("outer") // 2,
        "core": 2,
    }
    value_weight = value_weights(latent_out, out_grad, group)
    d_value_up = lax.psum_scatter(value_weight, axes, scatter_dimension=0, tiled=True)
    own_keys = jnp.concatenate([latent, key_rope, jnp.zeros_like(key_rope)], axis=1)
    own_keys, value_weight = lax.optimization_barrier((own_keys, value_weight))
    all_keys = gather_rows(own_keys, sizes).reshape(-1, WIDE)
    index = lax.iota(jnp.int32, blocks)
    held = (block_order[:, None] == index[None, :]).astype(jnp.int32)
    stored = jnp.sum(held * index[:, None], axis=0)
    first = 2 * lax.axis_index(axes)
    own = lax.dynamic_slice_in_dim(block_order, first, 2, 0)
    places = jnp.concatenate([own, stored])
    d_nope, d_rope, d_keys, key_weight = attention(
        places,
        query_nope,
        query_rope,
        all_keys,
        key_up,
        value_up,
        latent_out,
        out_grad,
        logsum,
        group,
    )
    d_key_up, own_sums = reduce_rows(key_weight, d_keys, sizes, 4)
    return (
        d_nope,
        d_rope,
        own_sums[:, :LATENT],
        own_sums[:, LATENT : LATENT + ROPE_DIM],
        d_key_up,
        d_value_up.astype(jnp.float32),
    )


def solution(mesh):
    placed = (
        P(("inner", "outer"), "head"),
        P(("inner", "outer"), "head"),
        P(("inner", "outer"), None),
        P(("inner", "outer"), None),
        P(None, "head"),
        P(None, "head"),
        P(("inner", "outer"), "head"),
        P(("inner", "outer"), "head"),
        P(("inner", "outer"), "head"),
        P(),
    )
    return jax.shard_map(
        local,
        mesh=mesh,
        in_specs=placed,
        out_specs=(
            P(("inner", "outer"), "head"),
            P(("inner", "outer"), "head"),
            P(("inner", "outer"), None),
            P(("inner", "outer"), None),
            P(("inner", "outer"), "head"),
            P(("inner", "outer"), "head"),
        ),
        check_vma=False,
    )
```

```python
import functools

import jax
import jax.numpy as jnp
from jax import lax
from jax.experimental import pallas as pl
from jax.experimental.pallas import tpu as pltpu
from jax.sharding import PartitionSpec as P

LATENT = 512
ROPE_DIM = 64
NOPE_DIM = 128
VALUE_DIM = 128
WIDE = 640
SPAN = 4
STORED = 2
FACTOR = float(NOPE_DIM + ROPE_DIM) ** (-0.5)
VMEM = 60 * 1024 * 1024


def contract_last(first_op, second_op):
    return lax.dot_general(
        first_op, second_op, (((1,), (1,)), ((), ())), preferred_element_type=jnp.float32
    )


def contract_first(first_op, second_op):
    return lax.dot_general(
        first_op, second_op, (((0,), (0,)), ((), ())), preferred_element_type=jnp.float32
    )


MESH = pl.DeviceIdType.MESH


def device_at(place, axis, value):
    head, inner, outer = place
    if axis == "head":
        return (value, inner, outer)
    if axis == "inner":
        return (head, value, outer)
    if axis == "depth":
        return (head, inner, value * 2 + lax.rem(outer, 2))
    return (head, inner, outer - lax.rem(outer, 2) + value)


def where_am_i():
    head, inner, outer = (lax.axis_index(a) for a in ("head", "inner", "outer"))
    spot = {"head": head, "inner": inner, "depth": outer // 2, "core": lax.rem(outer, 2)}
    return (head, inner, outer), spot


def greet(place, spot, sizes, axes):
    barrier = pltpu.get_barrier_semaphore()
    count = 0
    for axis in axes:
        for k in range(1, sizes[axis]):
            target = lax.rem(spot[axis] + k, sizes[axis])
            pl.semaphore_signal(
                barrier, inc=1, device_id=device_at(place, axis, target), device_id_type=MESH
            )
            count += 1
    pl.semaphore_wait(barrier, count)


def wide(x):
    return x.astype(jnp.float32)


def fused_kernel(
    sizes,
    group,
    block,
    blocks,
    places_ref,
    own_ref,
    nope_ref,
    rope_ref,
    key_up_ref,
    value_up_ref,
    saved_ref,
    upstream_ref,
    logsum_ref,
    d_nope_ref,
    d_rope_ref,
    d_latent_ref,
    d_key_rope_ref,
    d_key_up_ref,
    d_value_up_ref,
    gathered,
    keys,
    slots,
    queries,
    grads,
    delta,
    query_sums,
    w_part,
    w_recv1,
    w_recv2,
    w_sum2,
    w_recv3,
    k_part,
    k_recv1,
    k_recv2,
    k_sum2,
    k_recv3,
    k_sum3,
    k_recv4,
    k_own,
    g_depth,
    g_side,
    g_core,
    w1,
    w2,
    w3,
    k1,
    k2,
    k3,
    k4,
    k5,
):
    place, spot = where_am_i()
    depth, sides, heads = sizes["depth"], sizes["inner"], sizes["head"]
    inner, level, core, head = (spot[a] for a in ("inner", "depth", "core", "head"))
    rows = group * block
    tile = SPAN * block
    tiles = blocks // SPAN
    width = group * NOPE_DIM
    share = 2 * block // heads
    step = pl.program_id(0)
    steps = pl.num_programs(0)

    def remote(src, dst, axis, target, sems):
        return pltpu.make_async_remote_copy(
            src_ref=src,
            dst_ref=dst,
            send_sem=sems[0],
            recv_sem=sems[1],
            device_id=device_at(place, axis, target),
            device_id_type=MESH,
        )

    def partner(axis, k):
        return lax.rem(spot[axis] + k, sizes[axis])

    def both(sems, *index):
        return sems.at[(0,) + index], sems.at[(1,) + index]

    def owned(i, j, c):
        return pl.ds(2 * ((i * depth + j) * 2 + c), 2)

    def slot_copy(slot, axis, target, sems):
        both_blocks = gathered.at[owned(*slot)]
        return remote(both_blocks, both_blocks, axis, target, sems)

    def depth_key(k):
        return slot_copy((inner, level, core), "depth", partner("depth", k), both(g_depth, k - 1))

    def side_key(k, j):
        slot = (inner, lax.rem(level + depth - j, depth), core)
        return slot_copy(slot, "inner", partner("inner", k), both(g_side, k - 1, j))

    def core_key(k, j):
        slot = (lax.rem(inner + sides - k, sides), lax.rem(level + depth - j, depth), core)
        return slot_copy(slot, "core", 1 - core, both(g_core, k, j))

    def weight_core(kind, g):
        return remote(
            w_part.at[kind, g, :, :, 1 - core],
            w_recv1.at[kind, g],
            "core",
            1 - core,
            both(w1, kind, g),
        )

    def weight_side(kind, g, k):
        p = partner("inner", k)
        return remote(
            w_recv1.at[kind, g, p],
            w_recv2.at[kind, g, k - 1],
            "inner",
            p,
            both(w2, kind, g, k - 1),
        )

    def weight_depth(kind, g, k):
        p = partner("depth", k)
        return remote(
            w_sum2.at[kind, g, p],
            w_recv3.at[kind, g, k - 1],
            "depth",
            p,
            both(w3, kind, g, k - 1),
        )

    def start_weight(kind, g):
        weight_core(kind, g).start()

    def to_side(kind, g):
        weight_core(kind, g).wait_recv()
        for i in range(sides):
            for j in range(depth):
                total = wide(w_part[kind, g, i, j, core]) + wide(w_recv1[kind, g, i, j])
                w_recv1[kind, g, i, j] = total.astype(w_recv1.dtype)
        for k in range(1, sides):
            weight_side(kind, g, k).start()

    def to_depth(kind, g):
        for k in range(1, sides):
            weight_side(kind, g, k).wait_recv()
        for j in range(depth):
            total = wide(w_recv1[kind, g, inner, j])
            for k in range(sides - 1):
                total = total + wide(w_recv2[kind, g, k, j])
            w_sum2[kind, g, j] = total.astype(w_sum2.dtype)
        for k in range(1, depth):
            weight_depth(kind, g, k).start()

    def finish_weight(kind, g, out_ref):
        for k in range(1, depth):
            weight_depth(kind, g, k).wait_recv()
        total = wide(w_sum2[kind, g, level])
        for k in range(depth - 1):
            total = total + wide(w_recv3[kind, g, k])
        out_ref[:, pl.ds(pl.multiple_of(g * width, width), width)] = total

    def finish_sends(kind, g):
        weight_core(kind, g).wait_send()
        for k in range(1, sides):
            weight_side(kind, g, k).wait_send()
        for k in range(1, depth):
            weight_depth(kind, g, k).wait_send()

    def put_weight(kind, h, value):
        shaped = value.astype(w_part.dtype).reshape(w_part.shape[2:6] + (NOPE_DIM,))
        w_part[kind, step, :, :, :, :, h * NOPE_DIM : (h + 1) * NOPE_DIM] = shaped

    @pl.when(step == 0)
    def _():
        greet(place, spot, sizes, ("core", "depth", "inner", "head"))
        gathered[owned(inner, level, core)] = own_ref[...].reshape(2, block, WIDE)
        for k in range(1, depth):
            depth_key(k).start()
        for k in range(1, sides):
            side_key(k, 0).start()
        core_key(0, 0).start()
        slots[...] = jnp.zeros_like(slots)

    for h in range(group):
        saved = saved_ref[:, h * LATENT : (h + 1) * LATENT]
        upstream = upstream_ref[:, h * VALUE_DIM : (h + 1) * VALUE_DIM]
        put_weight(0, h, contract_first(saved, upstream))
    start_weight(0, step)

    @pl.when(step == 0)
    def _():
        for j in range(1, depth):
            depth_key(j).wait_recv()
            for k in range(1, sides):
                side_key(k, j).start()
            core_key(0, j).start()

    @pl.when(step > 0)
    def _():
        to_side(1, step - 1)

    query_sums[...] = jnp.zeros_like(query_sums)
    for h in range(group):
        nope = nope_ref[:, h * NOPE_DIM : (h + 1) * NOPE_DIM]
        key_map = key_up_ref[:, h * NOPE_DIM : (h + 1) * NOPE_DIM]
        lat = contract_last(nope, key_map).astype(jnp.bfloat16)
        upstream = upstream_ref[:, h * VALUE_DIM : (h + 1) * VALUE_DIM]
        value_map = value_up_ref[:, h * VALUE_DIM : (h + 1) * VALUE_DIM]
        grad = contract_last(upstream, value_map).astype(jnp.bfloat16)
        for t in range(2):
            mine = slice(h * block, (h + 1) * block)
            held = slice(t * block, (t + 1) * block)
            queries[t, mine, :LATENT] = lat[held]
            part = rope_ref[held, h * ROPE_DIM : (h + 1) * ROPE_DIM]
            queries[t, mine, LATENT:] = jnp.concatenate([part, jnp.zeros_like(part)], axis=1)
            grads[t, mine, :] = grad[held]
    for t in range(2):
        held = slice(t * block, (t + 1) * block)
        for h in range(0, group, 2):
            saved = jnp.concatenate(
                [saved_ref[held, k * LATENT : (k + 1) * LATENT] for k in (h, h + 1)], axis=0
            )
            mine = slice(h * block, (h + 2) * block)
            product = wide(grads[t, mine, :]) * wide(saved)
            folded = product[:, :128]
            for k in range(128, LATENT, 128):
                folded = folded + product[:, k : k + 128]
            delta[t, :, mine] = jnp.sum(folded.T, axis=0, keepdims=True)

    @pl.when(step == 0)
    def _():
        for j in range(depth):
            for k in range(1, sides):
                side_key(k, j).wait_recv()
                core_key(k, j).start()
        for j in range(depth):
            for k in range(sides):
                core_key(k, j).wait_recv()

        def sort(p, carry):
            for k in range(SPAN):
                keys[p, k * block : (k + 1) * block, :] = gathered[
                    places_ref[STORED + p * SPAN + k]
                ]
            return carry

        lax.fori_loop(0, tiles, sort, 0)

    to_side(0, step)

    span = tiles + 1
    base = STORED + 2 * blocks
    late = places_ref[0]
    early = places_ref[1]
    key_index = lax.broadcasted_iota(jnp.int32, (tile, rows), 0)
    row_index = lax.rem(lax.broadcasted_iota(jnp.int32, (tile, rows), 1), block)
    apart = key_index - row_index

    def visit(i, carry):
        target = places_ref[base + i]
        upper = jnp.broadcast_to(places_ref[base + span + i], (rows, WIDE)) > 0
        query = queries[target]
        grad = grads[target]
        held = keys[places_ref[base + 2 * span + i]]
        scores = contract_last(held, query) * FACTOR
        visible = apart <= places_ref[base + 3 * span + i]
        weights = jnp.where(visible, jnp.exp(scores - logsum_ref[target]), 0.0)
        dprobs = contract_last(held[:, :LATENT], grad)
        dscore = (weights * (dprobs - delta[target]) * FACTOR).astype(jnp.bfloat16)
        rounded = weights.astype(jnp.bfloat16)
        from_keys = contract_first(dscore, held)
        query_sums[0] += jnp.where(upper, from_keys, 0.0)
        query_sums[1] += jnp.where(upper, 0.0, from_keys)
        from_scores = jnp.dot(dscore, query, preferred_element_type=jnp.float32)
        from_values = jnp.dot(rounded, grad, preferred_element_type=jnp.float32)
        mine = pl.ds(i * SPAN, SPAN)
        from_scores = from_scores.reshape(SPAN, block, WIDE)
        from_values = from_values.reshape(SPAN, block, LATENT)
        slots[mine, :, :LATENT] += from_scores[:, :, :LATENT] + from_values
        slots[mine, :, LATENT:] += from_scores[:, :, LATENT:]
        return carry

    lax.fori_loop(0, tiles + 1, visit, 0)

    to_depth(0, step)

    @pl.when(step > 0)
    def _():
        to_depth(1, step - 1)

    for h in range(group):
        mine = slice(h * block, (h + 1) * block)
        cols = slice(h * NOPE_DIM, (h + 1) * NOPE_DIM)
        halves = [query_sums[late, mine, :], query_sums[early, mine, :]]
        grad_query = jnp.concatenate([x[:, :LATENT] for x in halves], axis=0)
        grad_query = grad_query.astype(jnp.bfloat16)
        d_nope_ref[:, cols] = jnp.dot(
            grad_query, key_up_ref[:, cols], preferred_element_type=jnp.float32
        ).astype(jnp.bfloat16)
        put_weight(1, h, contract_first(grad_query, nope_ref[:, cols]))
    start_weight(1, step)
    for t in range(2):
        held = slice(t * block, (t + 1) * block)
        source = late if t == 0 else early
        for h in range(0, group, 2):
            pair = [
                query_sums[source, k * block : (k + 1) * block, LATENT:][:, :ROPE_DIM]
                for k in (h, h + 1)
            ]
            d_rope_ref[held, h * ROPE_DIM : (h + 2) * ROPE_DIM] = jnp.concatenate(
                pair, axis=1
            ).astype(jnp.bfloat16)

    @pl.when(step == steps - 1)
    def _():
        def chosen(at):
            return jnp.broadcast_to(places_ref[at], (SPAN, block, WIDE)) > 0

        def combine(t, carry):
            here = pl.ds(t * SPAN, SPAN)
            there = pl.ds((tiles - 1 - t) * SPAN, SPAN)
            other = slots[there]
            above = chosen(base + 4 * span + t)
            lowest = chosen(base + 5 * span + t)
            slots[here] = (
                slots[here]
                + jnp.where(above, other, 0.0)
                + jnp.where(lowest, slots[tiles * SPAN :], 0.0)
            )
            slots[there] = jnp.where(above, 0.0, other)
            return carry

        lax.fori_loop(0, tiles // 2, combine, 0)

        for i in range(sides):

            def restore(j, carry):
                for c in range(2):
                    for half in range(2):
                        b = ((i * depth + j) * 2 + c) * 2 + half
                        k_part[i, j, c, half * block : (half + 1) * block, :] = slots[
                            places_ref[STORED + blocks + b]
                        ].astype(k_part.dtype)
                return carry

            lax.fori_loop(0, depth, restore, 0)

        def rows_of(target):
            return pl.ds(pl.multiple_of(target * share, share), share)

        keys_core = remote(k_part.at[:, :, 1 - core], k_recv1, "core", 1 - core, both(k1))
        keys_core.start()
        keys_core.wait_recv()
        for i in range(sides):
            for j in range(depth):
                total = wide(k_part[i, j, core]) + wide(k_recv1[i, j])
                k_recv1[i, j] = total.astype(k_recv1.dtype)
        keys_head = [
            remote(
                k_recv1.at[:, :, rows_of(partner("head", k)), :],
                k_recv2.at[k - 1],
                "head",
                partner("head", k),
                both(k2, k - 1),
            )
            for k in range(1, heads)
        ]
        for copy in keys_head:
            copy.start()
        to_side(1, step)
        for copy in keys_head:
            copy.wait_recv()
        for i in range(sides):
            for j in range(depth):
                total = wide(k_recv1[i, j, rows_of(head), :])
                for k in range(heads - 1):
                    total = total + wide(k_recv2[k, i, j])
                k_sum2[i, j] = total.astype(k_sum2.dtype)
        keys_side = [
            remote(
                k_sum2.at[partner("inner", k)],
                k_recv3.at[k - 1],
                "inner",
                partner("inner", k),
                both(k3, k - 1),
            )
            for k in range(1, sides)
        ]
        for copy in keys_side:
            copy.start()
        to_depth(1, step)
        for copy in keys_side:
            copy.wait_recv()
        for j in range(depth):
            total = wide(k_sum2[inner, j])
            for k in range(sides - 1):
                total = total + wide(k_recv3[k, j])
            k_sum3[j] = total.astype(k_sum3.dtype)
        keys_depth = [
            remote(
                k_sum3.at[partner("depth", k)],
                k_recv4.at[k - 1],
                "depth",
                partner("depth", k),
                both(k4, k - 1),
            )
            for k in range(1, depth)
        ]
        for copy in keys_depth:
            copy.start()

        def finish(g, carry):
            finish_weight(0, g, d_value_up_ref)
            finish_weight(1, g, d_key_up_ref)
            return carry

        lax.fori_loop(0, steps, finish, 0)
        for copy in keys_depth:
            copy.wait_recv()
        total = wide(k_sum3[level])
        for k in range(depth - 1):
            total = total + wide(k_recv4[k])
        k_own[rows_of(head), :] = total.astype(k_own.dtype)
        keys_last = [
            remote(
                k_own.at[rows_of(head), :],
                k_own.at[rows_of(head), :],
                "head",
                partner("head", k),
                both(k5, k - 1),
            )
            for k in range(1, heads)
        ]
        for copy in keys_last:
            copy.start()

        def drain(g, carry):
            finish_sends(0, g)
            finish_sends(1, g)
            return carry

        lax.fori_loop(0, steps, drain, 0)
        for k in range(1, depth):
            depth_key(k).wait_send()
        for j in range(depth):
            for k in range(1, sides):
                side_key(k, j).wait_send()
            for k in range(sides):
                core_key(k, j).wait_send()
        for copy in [keys_core] + keys_head + keys_side + keys_depth:
            copy.wait_send()
        for copy in keys_last:
            copy.wait()
        d_latent_ref[...] = k_own[:, :LATENT]
        d_key_rope_ref[...] = k_own[:, LATENT:][:, :ROPE_DIM]


def fused(
    sizes,
    group,
    places,
    own_keys,
    query_nope,
    query_rope,
    key_up,
    value_up,
    saved,
    upstream,
    logsum,
):
    depth, sides, heads = sizes["depth"], sizes["inner"], sizes["head"]
    owners = sides * depth * 2
    tokens = query_nope.shape[0]
    local_heads = query_nope.shape[1] // NOPE_DIM
    steps = local_heads // group
    block = tokens // 2
    length = owners * tokens
    blocks = length // block
    rows = group * block
    share = LATENT // owners
    totals = logsum.reshape(2, block, local_heads).transpose(0, 2, 1)
    totals = totals.reshape(2, 1, local_heads * block)
    whole = lambda i: (0, 0)
    part = lambda i: (0, i)
    narrow = lambda *shape: pltpu.VMEM(shape, jnp.bfloat16)
    full = lambda *shape: pltpu.VMEM(shape, jnp.float32)
    dma = lambda *shape: pltpu.SemaphoreType.DMA(shape)
    piece = (share, group * NOPE_DIM)
    mine = (tokens, WIDE)
    split = (tokens // heads, WIDE)
    pairs = length * local_heads * tokens // 2
    return pl.pallas_call(
        functools.partial(fused_kernel, sizes, group, block, blocks),
        grid=(steps,),
        in_specs=[
            pl.BlockSpec(memory_space=pltpu.SMEM),
            pl.BlockSpec(mine, whole),
            pl.BlockSpec((tokens, group * NOPE_DIM), part),
            pl.BlockSpec((tokens, group * ROPE_DIM), part),
            pl.BlockSpec((LATENT, group * NOPE_DIM), part),
            pl.BlockSpec((LATENT, group * VALUE_DIM), part),
            pl.BlockSpec((tokens, group * LATENT), part),
            pl.BlockSpec((tokens, group * VALUE_DIM), part),
            pl.BlockSpec((2, 1, rows), lambda i: (0, 0, i)),
        ],
        out_specs=[
            pl.BlockSpec((tokens, group * NOPE_DIM), part),
            pl.BlockSpec((tokens, group * ROPE_DIM), part),
            pl.BlockSpec((tokens, LATENT), whole),
            pl.BlockSpec((tokens, ROPE_DIM), whole),
            pl.BlockSpec((share, local_heads * NOPE_DIM), whole),
            pl.BlockSpec((share, local_heads * VALUE_DIM), whole),
        ],
        scratch_shapes=[
            narrow(blocks, block, WIDE),
            narrow(blocks // SPAN, SPAN * block, WIDE),
            full(blocks + SPAN, block, WIDE),
            narrow(2, rows, WIDE),
            narrow(2, rows, LATENT),
            full(2, 1, rows),
            full(2, rows, WIDE),
            narrow(2, steps, sides, depth, 2, *piece),
            narrow(2, steps, sides, depth, *piece),
            narrow(2, steps, sides - 1, depth, *piece),
            narrow(2, steps, depth, *piece),
            narrow(2, steps, depth - 1, *piece),
            narrow(sides, depth, 2, *mine),
            narrow(sides, depth, *mine),
            narrow(heads - 1, sides, depth, *split),
            narrow(sides, depth, *split),
            narrow(sides - 1, depth, *split),
            narrow(depth, *split),
            narrow(depth - 1, *split),
            narrow(*mine),
            dma(2, depth - 1),
            dma(2, sides - 1, depth),
            dma(2, sides, depth),
            dma(2, 2, steps),
            dma(2, 2, steps, sides - 1),
            dma(2, 2, steps, depth - 1),
            dma(2),
            dma(2, heads - 1),
            dma(2, sides - 1),
            dma(2, depth - 1),
            dma(2, heads - 1),
        ],
        out_shape=[
            jax.ShapeDtypeStruct(query_nope.shape, jnp.bfloat16),
            jax.ShapeDtypeStruct(query_rope.shape, jnp.bfloat16),
            jax.ShapeDtypeStruct((tokens, LATENT), jnp.bfloat16),
            jax.ShapeDtypeStruct((tokens, ROPE_DIM), jnp.bfloat16),
            jax.ShapeDtypeStruct((share, local_heads * NOPE_DIM), jnp.float32),
            jax.ShapeDtypeStruct((share, local_heads * VALUE_DIM), jnp.float32),
        ],
        compiler_params=pltpu.CompilerParams(
            collective_id=0, has_side_effects=True, vmem_limit_bytes=VMEM
        ),
        cost_estimate=pl.CostEstimate(
            flops=pairs * 2 * 2752, bytes_accessed=20 * 1024 * 1024, transcendentals=pairs
        ),
        name="latent_attention_backward",
    )(places, own_keys, query_nope, query_rope, key_up, value_up, saved, upstream, totals)


def local(
    query_nope,
    query_rope,
    latent,
    key_rope,
    key_up,
    value_up,
    latent_out,
    out_grad,
    logsum,
    block_order,
):
    axes = ("inner", "outer")
    heads = query_nope.shape[1] // NOPE_DIM
    blocks = block_order.shape[0]
    group = min(8, heads)
    sizes = {
        "head": lax.axis_size("head"),
        "inner": lax.axis_size("inner"),
        "depth": lax.axis_size("outer") // 2,
        "core": 2,
    }
    own_keys = jnp.concatenate([latent, key_rope, jnp.zeros_like(key_rope)], axis=1)
    index = lax.iota(jnp.int32, blocks)
    held = (block_order[:, None] == index[None, :]).astype(jnp.int32)
    stored = jnp.sum(held * index[:, None], axis=0)
    own = lax.dynamic_slice_in_dim(block_order, 2 * lax.axis_index(axes), 2, 0)
    tiles = blocks // SPAN
    late = (own[1] > own[0]).astype(jnp.int32)
    later, earlier = jnp.max(own), jnp.min(own)
    top, low = later // SPAN, earlier // SPAN
    slot = lax.iota(jnp.int32, tiles + 1)
    upper = (slot <= jnp.minimum(top, tiles - 1)).astype(jnp.int32)
    lower_tile = jnp.where(slot == tiles, low, tiles - 1 - slot)
    tile_of = jnp.where(upper > 0, slot, lower_tile)
    limit = jnp.where(upper > 0, later, earlier) - tile_of * SPAN
    places = jnp.concatenate(
        [
            jnp.stack([late, 1 - late]),
            stored,
            block_order,
            jnp.where(upper > 0, late, 1 - late),
            upper,
            tile_of,
            limit * (query_nope.shape[0] // 2),
            (tiles - 1 - slot > top).astype(jnp.int32),
            (slot == low).astype(jnp.int32),
        ]
    )
    return fused(
        sizes,
        group,
        places,
        own_keys,
        query_nope,
        query_rope,
        key_up,
        value_up,
        latent_out,
        out_grad,
        logsum,
    )


def solution(mesh):
    placed = (
        P(("inner", "outer"), "head"),
        P(("inner", "outer"), "head"),
        P(("inner", "outer"), None),
        P(("inner", "outer"), None),
        P(None, "head"),
        P(None, "head"),
        P(("inner", "outer"), "head"),
        P(("inner", "outer"), "head"),
        P(("inner", "outer"), "head"),
        P(),
    )
    return jax.shard_map(
        local,
        mesh=mesh,
        in_specs=placed,
        out_specs=(
            P(("inner", "outer"), "head"),
            P(("inner", "outer"), "head"),
            P(("inner", "outer"), None),
            P(("inner", "outer"), None),
            P(("inner", "outer"), "head"),
            P(("inner", "outer"), "head"),
        ),
        check_vma=False,
    )
```

```python
import functools

import jax
import jax.numpy as jnp
import numpy as np
from jax import lax
from jax.experimental import pallas as pl
from jax.experimental.pallas import tpu as pltpu
from jax.sharding import PartitionSpec as P

LATENT = 512
ROPE_DIM = 64
NOPE_DIM = 128
VALUE_DIM = 128
WIDE = 640
PIECE = 128
SPAN = 4
FIELDS = 7
FACTOR = float(NOPE_DIM + ROPE_DIM) ** (-0.5)
VMEM = 60 * 1024 * 1024


def contract_last(first_op, second_op):
    return lax.dot_general(
        first_op, second_op, (((1,), (1,)), ((), ())), preferred_element_type=jnp.float32
    )


def contract_first(first_op, second_op):
    return lax.dot_general(
        first_op, second_op, (((0,), (0,)), ((), ())), preferred_element_type=jnp.float32
    )


MESH = pl.DeviceIdType.MESH


def device_at(place, axis, value):
    head, inner, outer = place
    if axis == "head":
        return (value, inner, outer)
    if axis == "inner":
        return (head, value, outer)
    if axis == "depth":
        return (head, inner, value * 2 + lax.rem(outer, 2))
    return (head, inner, outer - lax.rem(outer, 2) + value)


def where_am_i():
    head, inner, outer = (lax.axis_index(a) for a in ("head", "inner", "outer"))
    spot = {"head": head, "inner": inner, "depth": outer // 2, "core": lax.rem(outer, 2)}
    return (head, inner, outer), spot


def greet(place, spot, sizes, axes):
    barrier = pltpu.get_barrier_semaphore()
    count = 0
    for axis in axes:
        for k in range(1, sizes[axis]):
            target = lax.rem(spot[axis] + k, sizes[axis])
            pl.semaphore_signal(
                barrier, inc=1, device_id=device_at(place, axis, target), device_id_type=MESH
            )
            count += 1
    pl.semaphore_wait(barrier, count)


def wide(x):
    return x.astype(jnp.float32)


def fused_kernel(
    sizes,
    group,
    block,
    blocks,
    stored_ref,
    order_ref,
    table_ref,
    own_lat_ref,
    own_rope_ref,
    nope_ref,
    rope_ref,
    key_up_ref,
    value_up_ref,
    saved_ref,
    upstream_ref,
    logsum_ref,
    d_nope_ref,
    d_rope_ref,
    d_latent_ref,
    d_key_rope_ref,
    d_key_up_ref,
    d_value_up_ref,
    gathered,
    keys,
    slots,
    queries,
    grads,
    delta,
    query_sums,
    w_part,
    w_recv1,
    w_recv2,
    w_sum2,
    w_recv3,
    k_part,
    k_recv1,
    k_recv2,
    k_sum2,
    k_recv3,
    k_sum3,
    k_recv4,
    k_own,
    g_depth,
    g_side,
    g_core,
    w1,
    w2,
    w3,
    k1,
    k2,
    k3,
    k4,
    k5,
):
    place, spot = where_am_i()
    depth, sides, heads = sizes["depth"], sizes["inner"], sizes["head"]
    inner, level, core, head = (spot[a] for a in ("inner", "depth", "core", "head"))
    rows = group * block
    tile = SPAN * block
    tiles = blocks // SPAN
    width = group * NOPE_DIM
    share = 2 * block // heads
    span = tiles + 1
    me = (inner * depth + level) * 2 + core
    step = pl.program_id(0)
    steps = pl.num_programs(0)

    def remote(src, dst, axis, target, sems):
        return pltpu.make_async_remote_copy(
            src_ref=src,
            dst_ref=dst,
            send_sem=sems[0],
            recv_sem=sems[1],
            device_id=device_at(place, axis, target),
            device_id_type=MESH,
        )

    def partner(axis, k):
        return lax.rem(spot[axis] + k, sizes[axis])

    def both(sems, *index):
        return sems.at[(0,) + index], sems.at[(1,) + index]

    def owned(i, j, c):
        return pl.ds(2 * ((i * depth + j) * 2 + c), 2)

    def slot_copy(slot, axis, target, sems):
        both_blocks = gathered.at[owned(*slot)]
        return remote(both_blocks, both_blocks, axis, target, sems)

    def depth_key(k):
        return slot_copy((inner, level, core), "depth", partner("depth", k), both(g_depth, k - 1))

    def side_key(k, j):
        slot = (inner, lax.rem(level + depth - j, depth), core)
        return slot_copy(slot, "inner", partner("inner", k), both(g_side, k - 1, j))

    def core_key(k, j):
        slot = (lax.rem(inner + sides - k, sides), lax.rem(level + depth - j, depth), core)
        return slot_copy(slot, "core", 1 - core, both(g_core, k, j))

    def weight_core(kind, g):
        return remote(
            w_part.at[kind, g, :, :, 1 - core],
            w_recv1.at[kind, g],
            "core",
            1 - core,
            both(w1, kind, g),
        )

    def weight_side(kind, g, k):
        p = partner("inner", k)
        return remote(
            w_recv1.at[kind, g, p],
            w_recv2.at[kind, g, k - 1],
            "inner",
            p,
            both(w2, kind, g, k - 1),
        )

    def weight_depth(kind, g, k):
        p = partner("depth", k)
        return remote(
            w_sum2.at[kind, g, p],
            w_recv3.at[kind, g, k - 1],
            "depth",
            p,
            both(w3, kind, g, k - 1),
        )

    def start_weight(kind, g):
        weight_core(kind, g).start()

    def to_side(kind, g):
        weight_core(kind, g).wait_recv()
        for i in range(sides):
            for j in range(depth):
                total = wide(w_part[kind, g, i, j, core]) + wide(w_recv1[kind, g, i, j])
                w_recv1[kind, g, i, j] = total.astype(w_recv1.dtype)
        for k in range(1, sides):
            weight_side(kind, g, k).start()

    def to_depth(kind, g):
        for k in range(1, sides):
            weight_side(kind, g, k).wait_recv()
        for j in range(depth):
            total = wide(w_recv1[kind, g, inner, j])
            for k in range(sides - 1):
                total = total + wide(w_recv2[kind, g, k, j])
            w_sum2[kind, g, j] = total.astype(w_sum2.dtype)
        for k in range(1, depth):
            weight_depth(kind, g, k).start()

    def finish_weight(kind, g, out_ref):
        for k in range(1, depth):
            weight_depth(kind, g, k).wait_recv()
        total = wide(w_sum2[kind, g, level])
        for k in range(depth - 1):
            total = total + wide(w_recv3[kind, g, k])
        out_ref[:, pl.ds(pl.multiple_of(g * width, width), width)] = total

    def finish_sends(kind, g):
        weight_core(kind, g).wait_send()
        for k in range(1, sides):
            weight_side(kind, g, k).wait_send()
        for k in range(1, depth):
            weight_depth(kind, g, k).wait_send()

    def put_weight(kind, h, value):
        shaped = value.astype(w_part.dtype).reshape(w_part.shape[2:6] + (NOPE_DIM,))
        w_part[kind, step, :, :, :, :, h * NOPE_DIM : (h + 1) * NOPE_DIM] = shaped

    @pl.when(step == 0)
    def _():
        greet(place, spot, sizes, ("core", "depth", "inner", "head"))
        part = own_rope_ref[...]
        mine = owned(inner, level, core)
        gathered[mine, :, :LATENT] = own_lat_ref[...].reshape(2, block, LATENT)
        gathered[mine, :, LATENT:] = jnp.concatenate([part, jnp.zeros_like(part)], axis=1).reshape(
            2, block, WIDE - LATENT
        )
        for k in range(1, depth):
            depth_key(k).start()
        for k in range(1, sides):
            side_key(k, 0).start()
        core_key(0, 0).start()
        slots[...] = jnp.zeros_like(slots)

    for h in range(group):
        saved = saved_ref[:, h * LATENT : (h + 1) * LATENT]
        upstream = upstream_ref[:, h * VALUE_DIM : (h + 1) * VALUE_DIM]
        put_weight(0, h, contract_first(saved, upstream))
    start_weight(0, step)

    @pl.when(step == 0)
    def _():
        for j in range(1, depth):
            depth_key(j).wait_recv()
            for k in range(1, sides):
                side_key(k, j).start()
            core_key(0, j).start()

    @pl.when(step > 0)
    def _():
        to_side(1, step - 1)

    query_sums[...] = jnp.zeros_like(query_sums)
    for h in range(group):
        nope = nope_ref[:, h * NOPE_DIM : (h + 1) * NOPE_DIM]
        key_map = key_up_ref[:, h * NOPE_DIM : (h + 1) * NOPE_DIM]
        lat = contract_last(nope, key_map).astype(jnp.bfloat16)
        upstream = upstream_ref[:, h * VALUE_DIM : (h + 1) * VALUE_DIM]
        value_map = value_up_ref[:, h * VALUE_DIM : (h + 1) * VALUE_DIM]
        grad = contract_last(upstream, value_map).astype(jnp.bfloat16)
        for t in range(2):
            mine = slice(h * block, (h + 1) * block)
            held = slice(t * block, (t + 1) * block)
            queries[t, mine, :LATENT] = lat[held]
            part = rope_ref[held, h * ROPE_DIM : (h + 1) * ROPE_DIM]
            queries[t, mine, LATENT:] = jnp.concatenate([part, jnp.zeros_like(part)], axis=1)
            grads[t, mine, :] = grad[held]
    for t in range(2):
        held = slice(t * block, (t + 1) * block)
        for h in range(0, group, 2):
            saved = jnp.concatenate(
                [saved_ref[held, k * LATENT : (k + 1) * LATENT] for k in (h, h + 1)], axis=0
            )
            mine = slice(h * block, (h + 2) * block)
            product = wide(grads[t, mine, :]) * wide(saved)
            folded = product[:, :128]
            for k in range(128, LATENT, 128):
                folded = folded + product[:, k : k + 128]
            delta[t, :, mine] = jnp.sum(folded.T, axis=0, keepdims=True)

    @pl.when(step == 0)
    def _():
        for j in range(depth):
            for k in range(1, sides):
                side_key(k, j).wait_recv()
                core_key(k, j).start()
        for j in range(depth):
            for k in range(sides):
                core_key(k, j).wait_recv()

        def sort(p, carry):
            for k in range(SPAN):
                keys[p, k * block : (k + 1) * block, :] = gathered[
                    stored_ref[p * SPAN + k]
                ]
            return carry

        lax.fori_loop(0, tiles, sort, 0)

    to_side(0, step)

    late = table_ref[me, 6 * span]
    early = table_ref[me, 6 * span + 1]
    key_index = lax.broadcasted_iota(jnp.int32, (tile, rows), 0)
    row_index = lax.rem(lax.broadcasted_iota(jnp.int32, (tile, rows), 1), block)
    apart = key_index - row_index

    def visit(shared, i, carry):
        target = table_ref[me, i]
        query = queries[target]
        grad = grads[target]
        held = keys[table_ref[me, 2 * span + i]]
        scores = contract_last(held, query) * FACTOR
        visible = apart <= table_ref[me, 3 * span + i]
        weights = jnp.where(visible, jnp.exp(scores - logsum_ref[target]), 0.0)
        dprobs = contract_last(held[:, :LATENT], grad)
        dscore = (weights * (dprobs - delta[target]) * FACTOR).astype(jnp.bfloat16)
        rounded = weights.astype(jnp.bfloat16)
        from_keys = contract_first(dscore, held)
        if shared:
            upper = jnp.broadcast_to(table_ref[me, span + i], (rows, WIDE)) > 0
            query_sums[0] += jnp.where(upper, from_keys, 0.0)
            query_sums[1] += jnp.where(upper, 0.0, from_keys)
        else:
            query_sums[0] += from_keys
        from_scores = jnp.dot(dscore, query, preferred_element_type=jnp.float32)
        from_values = jnp.dot(rounded, grad, preferred_element_type=jnp.float32)
        mine = pl.ds(i * SPAN, SPAN)
        from_scores = from_scores.reshape(SPAN, block, WIDE)
        from_values = from_values.reshape(SPAN, block, LATENT)
        slots[mine, :, :LATENT] += from_scores[:, :, :LATENT] + from_values
        slots[mine, :, LATENT:] += from_scores[:, :, LATENT:]
        return carry

    lax.fori_loop(0, tiles // 2, functools.partial(visit, False), 0)
    lax.fori_loop(tiles // 2, tiles + 1, functools.partial(visit, True), 0)

    to_depth(0, step)

    @pl.when(step > 0)
    def _():
        to_depth(1, step - 1)

    for h in range(group):
        mine = slice(h * block, (h + 1) * block)
        cols = slice(h * NOPE_DIM, (h + 1) * NOPE_DIM)
        halves = [query_sums[late, mine, :], query_sums[early, mine, :]]
        grad_query = jnp.concatenate([x[:, :LATENT] for x in halves], axis=0)
        grad_query = grad_query.astype(jnp.bfloat16)
        d_nope_ref[:, cols] = jnp.dot(
            grad_query, key_up_ref[:, cols], preferred_element_type=jnp.float32
        ).astype(jnp.bfloat16)
        put_weight(1, h, contract_first(grad_query, nope_ref[:, cols]))
    start_weight(1, step)
    for t in range(2):
        held = slice(t * block, (t + 1) * block)
        source = late if t == 0 else early
        for h in range(0, group, 2):
            pair = [
                query_sums[source, k * block : (k + 1) * block, LATENT:][:, :ROPE_DIM]
                for k in (h, h + 1)
            ]
            d_rope_ref[held, h * ROPE_DIM : (h + 2) * ROPE_DIM] = jnp.concatenate(
                pair, axis=1
            ).astype(jnp.bfloat16)

    @pl.when(step == steps - 1)
    def _():
        def chosen(at):
            return jnp.broadcast_to(table_ref[me, at], (SPAN, block, WIDE)) > 0

        def combine(t, carry):
            here = pl.ds(t * SPAN, SPAN)
            there = pl.ds((tiles - 1 - t) * SPAN, SPAN)
            other = slots[there]
            above = chosen(4 * span + t)
            lowest = chosen(5 * span + t)
            slots[here] = (
                slots[here]
                + jnp.where(above, other, 0.0)
                + jnp.where(lowest, slots[tiles * SPAN :], 0.0)
            )
            slots[there] = jnp.where(above, 0.0, other)
            return carry

        lax.fori_loop(0, tiles // 2, combine, 0)

        for i in range(sides):

            def restore(j, carry):
                for c in range(2):
                    for half in range(2):
                        b = ((i * depth + j) * 2 + c) * 2 + half
                        k_part[i, j, c, half * block : (half + 1) * block, :] = slots[
                            order_ref[b]
                        ].astype(k_part.dtype)
                return carry

            lax.fori_loop(0, depth, restore, 0)

        def rows_of(target):
            return pl.ds(pl.multiple_of(target * share, share), share)

        pieces = WIDE // PIECE
        cols = [slice(c * PIECE, (c + 1) * PIECE) for c in range(pieces)]
        keys_core = [
            remote(
                k_part.at[:, :, 1 - core, :, cols[c]],
                k_recv1.at[c],
                "core",
                1 - core,
                both(k1, c),
            )
            for c in range(pieces)
        ]
        for copy in keys_core:
            copy.start()
        keys_head, keys_side, keys_depth = [], [], []
        for c in range(pieces):
            keys_core[c].wait_recv()
            for i in range(sides):
                for j in range(depth):
                    total = wide(k_part[i, j, core, :, cols[c]]) + wide(k_recv1[c, i, j])
                    k_recv1[c, i, j] = total.astype(k_recv1.dtype)
            copies = [
                remote(
                    k_recv1.at[c, :, :, rows_of(partner("head", k)), :],
                    k_recv2.at[c, k - 1],
                    "head",
                    partner("head", k),
                    both(k2, c, k - 1),
                )
                for k in range(1, heads)
            ]
            for copy in copies:
                copy.start()
            keys_head.append(copies)
        to_side(1, step)

        def head_to_side(c):
            for copy in keys_head[c]:
                copy.wait_recv()
            for i in range(sides):
                for j in range(depth):
                    total = wide(k_recv1[c, i, j, rows_of(head), :])
                    for k in range(heads - 1):
                        total = total + wide(k_recv2[c, k, i, j])
                    k_sum2[c, i, j] = total.astype(k_sum2.dtype)
            copies = [
                remote(
                    k_sum2.at[c, partner("inner", k)],
                    k_recv3.at[c, k - 1],
                    "inner",
                    partner("inner", k),
                    both(k3, c, k - 1),
                )
                for k in range(1, sides)
            ]
            for copy in copies:
                copy.start()
            keys_side.append(copies)

        def side_to_depth(c):
            for copy in keys_side[c]:
                copy.wait_recv()
            for j in range(depth):
                total = wide(k_sum2[c, inner, j])
                for k in range(sides - 1):
                    total = total + wide(k_recv3[c, k, j])
                k_sum3[c, j] = total.astype(k_sum3.dtype)
            copies = [
                remote(
                    k_sum3.at[c, partner("depth", k)],
                    k_recv4.at[c, k - 1],
                    "depth",
                    partner("depth", k),
                    both(k4, c, k - 1),
                )
                for k in range(1, depth)
            ]
            for copy in copies:
                copy.start()
            keys_depth.append(copies)

        for c in range(pieces):
            head_to_side(c)
            if c == 1:
                to_depth(1, step)
            if c > 0:
                side_to_depth(c - 1)
        side_to_depth(pieces - 1)

        def finish(g, carry):
            finish_weight(0, g, d_value_up_ref)
            finish_weight(1, g, d_key_up_ref)
            return carry

        lax.fori_loop(0, steps, finish, 0)
        for c in range(pieces):
            for copy in keys_depth[c]:
                copy.wait_recv()
            total = wide(k_sum3[c, level])
            for k in range(depth - 1):
                total = total + wide(k_recv4[c, k])
            k_own[rows_of(head), cols[c]] = total.astype(k_own.dtype)
        keys_last = [
            remote(
                k_own.at[rows_of(head), :],
                k_own.at[rows_of(head), :],
                "head",
                partner("head", k),
                both(k5, k - 1),
            )
            for k in range(1, heads)
        ]
        for copy in keys_last:
            copy.start()

        def drain(g, carry):
            finish_sends(0, g)
            finish_sends(1, g)
            return carry

        lax.fori_loop(0, steps, drain, 0)
        for k in range(1, depth):
            depth_key(k).wait_send()
        for j in range(depth):
            for k in range(1, sides):
                side_key(k, j).wait_send()
            for k in range(sides):
                core_key(k, j).wait_send()
        for copy in keys_core + sum(keys_head + keys_side + keys_depth, []):
            copy.wait_send()
        for copy in keys_last:
            copy.wait()
        d_latent_ref[...] = k_own[:, :LATENT]
        d_key_rope_ref[...] = k_own[:, LATENT:][:, :ROPE_DIM]


def fused(
    sizes,
    group,
    stored,
    order,
    table,
    latent,
    key_rope,
    query_nope,
    query_rope,
    key_up,
    value_up,
    saved,
    upstream,
    logsum,
):
    depth, sides, heads = sizes["depth"], sizes["inner"], sizes["head"]
    owners = sides * depth * 2
    tokens = query_nope.shape[0]
    local_heads = query_nope.shape[1] // NOPE_DIM
    steps = local_heads // group
    block = tokens // 2
    length = owners * tokens
    blocks = length // block
    rows = group * block
    share = LATENT // owners
    totals = logsum.reshape(2, block, local_heads).transpose(0, 2, 1)
    totals = totals.reshape(2, 1, local_heads * block)
    whole = lambda i: (0, 0)
    part = lambda i: (0, i)
    narrow = lambda *shape: pltpu.VMEM(shape, jnp.bfloat16)
    full = lambda *shape: pltpu.VMEM(shape, jnp.float32)
    dma = lambda *shape: pltpu.SemaphoreType.DMA(shape)
    piece = (share, group * NOPE_DIM)
    mine = (tokens, WIDE)
    split = (tokens // heads, PIECE)
    pieces = WIDE // PIECE
    pairs = length * local_heads * tokens // 2
    results = pl.pallas_call(
        functools.partial(fused_kernel, sizes, group, block, blocks),
        grid=(steps,),
        in_specs=[
            pl.BlockSpec(memory_space=pltpu.SMEM),
            pl.BlockSpec(memory_space=pltpu.SMEM),
            pl.BlockSpec(memory_space=pltpu.SMEM),
            pl.BlockSpec((tokens, LATENT), whole),
            pl.BlockSpec((tokens, ROPE_DIM), whole),
            pl.BlockSpec((tokens, group * NOPE_DIM), part),
            pl.BlockSpec((tokens, group * ROPE_DIM), part),
            pl.BlockSpec((LATENT, group * NOPE_DIM), part),
            pl.BlockSpec((LATENT, group * VALUE_DIM), part),
            pl.BlockSpec((tokens, group * LATENT), part),
            pl.BlockSpec((tokens, group * VALUE_DIM), part),
            pl.BlockSpec((2, 1, rows), lambda i: (0, 0, i)),
        ],
        out_specs=[
            pl.BlockSpec((tokens, group * NOPE_DIM), part),
            pl.BlockSpec((tokens, group * ROPE_DIM), part),
            pl.BlockSpec((tokens, LATENT), whole),
            pl.BlockSpec((tokens, ROPE_DIM), whole),
            pl.BlockSpec((share, local_heads * NOPE_DIM), whole),
            pl.BlockSpec((share, local_heads * VALUE_DIM), whole),
        ],
        scratch_shapes=[
            narrow(blocks, block, WIDE),
            narrow(blocks // SPAN, SPAN * block, WIDE),
            full(blocks + SPAN, block, WIDE),
            narrow(2, rows, WIDE),
            narrow(2, rows, LATENT),
            full(2, 1, rows),
            full(2, rows, WIDE),
            narrow(2, steps, sides, depth, 2, *piece),
            narrow(2, steps, sides, depth, *piece),
            narrow(2, steps, sides - 1, depth, *piece),
            narrow(2, steps, depth, *piece),
            narrow(2, steps, depth - 1, *piece),
            narrow(sides, depth, 2, *mine),
            narrow(pieces, sides, depth, tokens, PIECE),
            narrow(pieces, heads - 1, sides, depth, *split),
            narrow(pieces, sides, depth, *split),
            narrow(pieces, sides - 1, depth, *split),
            narrow(pieces, depth, *split),
            narrow(pieces, depth - 1, *split),
            narrow(*mine),
            dma(2, depth - 1),
            dma(2, sides - 1, depth),
            dma(2, sides, depth),
            dma(2, 2, steps),
            dma(2, 2, steps, sides - 1),
            dma(2, 2, steps, depth - 1),
            dma(2, pieces),
            dma(2, pieces, heads - 1),
            dma(2, pieces, sides - 1),
            dma(2, pieces, depth - 1),
            dma(2, heads - 1),
        ],
        out_shape=[
            jax.ShapeDtypeStruct(query_nope.shape, jnp.bfloat16),
            jax.ShapeDtypeStruct(query_rope.shape, jnp.bfloat16),
            jax.ShapeDtypeStruct((tokens, LATENT), jnp.bfloat16),
            jax.ShapeDtypeStruct((tokens, ROPE_DIM), jnp.bfloat16),
            jax.ShapeDtypeStruct((share, local_heads * NOPE_DIM), jnp.float32),
            jax.ShapeDtypeStruct((share, local_heads * VALUE_DIM), jnp.float32),
        ],
        compiler_params=pltpu.CompilerParams(
            collective_id=0, has_side_effects=True, vmem_limit_bytes=VMEM
        ),
        cost_estimate=pl.CostEstimate(
            flops=pairs * 2 * 2752, bytes_accessed=20 * 1024 * 1024, transcendentals=pairs
        ),
        name="latent_attention_backward",
    )(
        stored,
        order,
        table,
        latent,
        key_rope,
        query_nope,
        query_rope,
        key_up,
        value_up,
        saved,
        upstream,
        totals,
    )
    return hand_over(results)


def hand_over_kernel(count, *refs):
    sems = refs[-1]
    copies = [
        pltpu.make_async_copy(refs[i], refs[count + i], sems.at[i]) for i in range(count)
    ]
    for copy in copies:
        copy.start()
    for copy in copies:
        copy.wait()


def hand_over(arrays):
    count = len(arrays)
    return pl.pallas_call(
        functools.partial(hand_over_kernel, count),
        in_specs=[pl.BlockSpec(memory_space=pl.ANY)] * count,
        out_specs=[pl.BlockSpec(memory_space=pl.ANY)] * count,
        out_shape=[jax.ShapeDtypeStruct(x.shape, x.dtype) for x in arrays],
        scratch_shapes=[pltpu.SemaphoreType.DMA((count,))],
        name="hand_over",
    )(*arrays)


def local(
    query_nope,
    query_rope,
    latent,
    key_rope,
    key_up,
    value_up,
    latent_out,
    out_grad,
    logsum,
    block_order,
):
    axes = ("inner", "outer")
    heads = query_nope.shape[1] // NOPE_DIM
    blocks = block_order.shape[0]
    group = min(8, heads)
    sizes = {
        "head": lax.axis_size("head"),
        "inner": lax.axis_size("inner"),
        "depth": lax.axis_size("outer") // 2,
        "core": 2,
    }
    index = lax.iota(jnp.int32, blocks)
    held = (block_order[:, None] == index[None, :]).astype(jnp.int32)
    stored = jnp.sum(held * index[:, None], axis=0)
    tiles = blocks // SPAN
    span = tiles + 1
    pair = block_order.reshape(-1, 2)
    first, second = pair[:, :1], pair[:, 1:]
    late = (second > first).astype(jnp.int32)
    later, earlier = jnp.maximum(first, second), jnp.minimum(first, second)
    top, low = later // SPAN, earlier // SPAN
    column = np.arange(FIELDS * span, dtype=np.int32)[None, :]
    field, slot = column // span, column % span
    upper = slot <= jnp.minimum(top, tiles - 1)
    tile_of = jnp.where(upper, slot, jnp.where(slot == tiles, low, tiles - 1 - slot))
    limit = (jnp.where(upper, later, earlier) - tile_of * SPAN) * (query_nope.shape[0] // 2)
    above = (tiles - 1 - slot > top).astype(jnp.int32)
    table = jnp.where(slot == 0, late, 1 - late)
    table = jnp.where(field == 5, (slot == low).astype(jnp.int32), table)
    table = jnp.where(field == 4, above, table)
    table = jnp.where(field == 3, limit, table)
    table = jnp.where(field == 2, tile_of, table)
    table = jnp.where(field == 1, upper.astype(jnp.int32), table)
    table = jnp.where(field == 0, jnp.where(upper, late, 1 - late), table)
    return fused(
        sizes,
        group,
        stored,
        block_order,
        table,
        latent,
        key_rope,
        query_nope,
        query_rope,
        key_up,
        value_up,
        latent_out,
        out_grad,
        logsum,
    )


def solution(mesh):
    placed = (
        P(("inner", "outer"), "head"),
        P(("inner", "outer"), "head"),
        P(("inner", "outer"), None),
        P(("inner", "outer"), None),
        P(None, "head"),
        P(None, "head"),
        P(("inner", "outer"), "head"),
        P(("inner", "outer"), "head"),
        P(("inner", "outer"), "head"),
        P(),
    )
    return jax.shard_map(
        local,
        mesh=mesh,
        in_specs=placed,
        out_specs=(
            P(("inner", "outer"), "head"),
            P(("inner", "outer"), "head"),
            P(("inner", "outer"), None),
            P(("inner", "outer"), None),
            P(("inner", "outer"), "head"),
            P(("inner", "outer"), "head"),
        ),
        check_vma=False,
    )
```

```python
import functools

import jax
import jax.numpy as jnp
import numpy as np
from jax import lax
from jax.experimental import pallas as pl
from jax.experimental.pallas import tpu as pltpu
from jax.sharding import PartitionSpec as P

LATENT = 512
ROPE_DIM = 64
NOPE_DIM = 128
VALUE_DIM = 128
WIDE = 640
PIECE = 128
SPAN = 4
FIELDS = 7
FACTOR = float(NOPE_DIM + ROPE_DIM) ** (-0.5)
VMEM = 60 * 1024 * 1024


def contract_last(first_op, second_op):
    return lax.dot_general(
        first_op, second_op, (((1,), (1,)), ((), ())), preferred_element_type=jnp.float32
    )


def contract_first(first_op, second_op):
    return lax.dot_general(
        first_op, second_op, (((0,), (0,)), ((), ())), preferred_element_type=jnp.float32
    )


MESH = pl.DeviceIdType.MESH


def device_at(place, axis, value):
    head, inner, outer = place
    if axis == "head":
        return (value, inner, outer)
    if axis == "inner":
        return (head, value, outer)
    if axis == "depth":
        return (head, inner, value * 2 + lax.rem(outer, 2))
    return (head, inner, outer - lax.rem(outer, 2) + value)


def where_am_i():
    head, inner, outer = (lax.axis_index(a) for a in ("head", "inner", "outer"))
    spot = {"head": head, "inner": inner, "depth": outer // 2, "core": lax.rem(outer, 2)}
    return (head, inner, outer), spot


def greet(place, spot, sizes, axes):
    barrier = pltpu.get_barrier_semaphore()
    count = 0
    for axis in axes:
        for k in range(1, sizes[axis]):
            target = lax.rem(spot[axis] + k, sizes[axis])
            pl.semaphore_signal(
                barrier, inc=1, device_id=device_at(place, axis, target), device_id_type=MESH
            )
            count += 1
    pl.semaphore_wait(barrier, count)


def wide(x):
    return x.astype(jnp.float32)


def fused_kernel(
    sizes,
    group,
    block,
    blocks,
    stored_ref,
    order_ref,
    table_ref,
    own_lat_ref,
    own_rope_ref,
    nope_ref,
    rope_ref,
    key_up_ref,
    value_up_ref,
    saved_ref,
    upstream_ref,
    logsum_ref,
    d_nope_ref,
    d_rope_ref,
    d_latent_ref,
    d_key_rope_ref,
    d_key_up_ref,
    d_value_up_ref,
    gathered,
    keys,
    slots,
    queries,
    grads,
    delta,
    query_sums,
    w_part,
    w_recv1,
    w_recv2,
    w_sum2,
    w_recv3,
    k_part,
    k_recv1,
    k_recv2,
    k_sum2,
    k_recv3,
    k_sum3,
    k_recv4,
    k_own,
    g_depth,
    g_side,
    g_core,
    w1,
    w2,
    w3,
    k1,
    k2,
    k3,
    k4,
    k5,
):
    place, spot = where_am_i()
    depth, sides, heads = sizes["depth"], sizes["inner"], sizes["head"]
    inner, level, core, head = (spot[a] for a in ("inner", "depth", "core", "head"))
    rows = group * block
    tile = SPAN * block
    tiles = blocks // SPAN
    width = group * NOPE_DIM
    share = 2 * block // heads
    span = tiles + 1
    me = (inner * depth + level) * 2 + core
    step = pl.program_id(0)
    steps = pl.num_programs(0)

    def remote(src, dst, axis, target, sems):
        return pltpu.make_async_remote_copy(
            src_ref=src,
            dst_ref=dst,
            send_sem=sems[0],
            recv_sem=sems[1],
            device_id=device_at(place, axis, target),
            device_id_type=MESH,
        )

    def partner(axis, k):
        return lax.rem(spot[axis] + k, sizes[axis])

    def both(sems, *index):
        return sems.at[(0,) + index], sems.at[(1,) + index]

    def owned(i, j, c):
        return pl.ds(2 * ((i * depth + j) * 2 + c), 2)

    def slot_copy(slot, axis, target, sems):
        both_blocks = gathered.at[owned(*slot)]
        return remote(both_blocks, both_blocks, axis, target, sems)

    def depth_key(k):
        return slot_copy((inner, level, core), "depth", partner("depth", k), both(g_depth, k - 1))

    def side_key(k, j):
        slot = (inner, lax.rem(level + depth - j, depth), core)
        return slot_copy(slot, "inner", partner("inner", k), both(g_side, k - 1, j))

    def core_key(k, j):
        slot = (lax.rem(inner + sides - k, sides), lax.rem(level + depth - j, depth), core)
        return slot_copy(slot, "core", 1 - core, both(g_core, k, j))

    def weight_core(kind, g):
        return remote(
            w_part.at[kind, g, :, :, 1 - core],
            w_recv1.at[kind, g],
            "core",
            1 - core,
            both(w1, kind, g),
        )

    def weight_side(kind, g, k):
        p = partner("inner", k)
        return remote(
            w_recv1.at[kind, g, p],
            w_recv2.at[kind, g, k - 1],
            "inner",
            p,
            both(w2, kind, g, k - 1),
        )

    def weight_depth(kind, g, k):
        p = partner("depth", k)
        return remote(
            w_sum2.at[kind, g, p],
            w_recv3.at[kind, g, k - 1],
            "depth",
            p,
            both(w3, kind, g, k - 1),
        )

    def start_weight(kind, g):
        weight_core(kind, g).start()

    def to_side(kind, g):
        weight_core(kind, g).wait_recv()
        for i in range(sides):
            for j in range(depth):
                total = wide(w_part[kind, g, i, j, core]) + wide(w_recv1[kind, g, i, j])
                w_recv1[kind, g, i, j] = total.astype(w_recv1.dtype)
        for k in range(1, sides):
            weight_side(kind, g, k).start()

    def to_depth(kind, g):
        for k in range(1, sides):
            weight_side(kind, g, k).wait_recv()
        for j in range(depth):
            total = wide(w_recv1[kind, g, inner, j])
            for k in range(sides - 1):
                total = total + wide(w_recv2[kind, g, k, j])
            w_sum2[kind, g, j] = total.astype(w_sum2.dtype)
        for k in range(1, depth):
            weight_depth(kind, g, k).start()

    def finish_weight(kind, g, out_ref):
        for k in range(1, depth):
            weight_depth(kind, g, k).wait_recv()
        total = wide(w_sum2[kind, g, level])
        for k in range(depth - 1):
            total = total + wide(w_recv3[kind, g, k])
        out_ref[:, pl.ds(pl.multiple_of(g * width, width), width)] = total

    def finish_sends(kind, g):
        weight_core(kind, g).wait_send()
        for k in range(1, sides):
            weight_side(kind, g, k).wait_send()
        for k in range(1, depth):
            weight_depth(kind, g, k).wait_send()

    def put_weight(kind, h, value):
        shaped = value.astype(w_part.dtype).reshape(w_part.shape[2:6] + (NOPE_DIM,))
        w_part[kind, step, :, :, :, :, h * NOPE_DIM : (h + 1) * NOPE_DIM] = shaped

    @pl.when(step == 0)
    def _():
        greet(place, spot, sizes, ("core", "depth", "inner", "head"))
        part = own_rope_ref[...]
        mine = owned(inner, level, core)
        gathered[mine, :, :LATENT] = own_lat_ref[...].reshape(2, block, LATENT)
        gathered[mine, :, LATENT:] = jnp.concatenate([part, jnp.zeros_like(part)], axis=1).reshape(
            2, block, WIDE - LATENT
        )
        for k in range(1, depth):
            depth_key(k).start()
        for k in range(1, sides):
            side_key(k, 0).start()
        core_key(0, 0).start()
        slots[...] = jnp.zeros_like(slots)

    for h in range(group):
        saved = saved_ref[:, h * LATENT : (h + 1) * LATENT]
        upstream = upstream_ref[:, h * VALUE_DIM : (h + 1) * VALUE_DIM]
        put_weight(0, h, contract_first(saved, upstream))
    start_weight(0, step)

    @pl.when(step == 0)
    def _():
        for j in range(1, depth):
            depth_key(j).wait_recv()
            for k in range(1, sides):
                side_key(k, j).start()
            core_key(0, j).start()

    @pl.when(step > 0)
    def _():
        to_side(1, step - 1)

    query_sums[...] = jnp.zeros_like(query_sums)
    for h in range(group):
        nope = nope_ref[:, h * NOPE_DIM : (h + 1) * NOPE_DIM]
        key_map = key_up_ref[:, h * NOPE_DIM : (h + 1) * NOPE_DIM]
        lat = contract_last(nope, key_map).astype(jnp.bfloat16)
        upstream = upstream_ref[:, h * VALUE_DIM : (h + 1) * VALUE_DIM]
        value_map = value_up_ref[:, h * VALUE_DIM : (h + 1) * VALUE_DIM]
        grad = contract_last(upstream, value_map).astype(jnp.bfloat16)
        for t in range(2):
            mine = slice(h * block, (h + 1) * block)
            held = slice(t * block, (t + 1) * block)
            queries[t, mine, :LATENT] = lat[held]
            part = rope_ref[held, h * ROPE_DIM : (h + 1) * ROPE_DIM]
            queries[t, mine, LATENT:] = jnp.concatenate([part, jnp.zeros_like(part)], axis=1)
            grads[t, mine, :] = grad[held]
    for t in range(2):
        held = slice(t * block, (t + 1) * block)
        for h in range(0, group, 2):
            saved = jnp.concatenate(
                [saved_ref[held, k * LATENT : (k + 1) * LATENT] for k in (h, h + 1)], axis=0
            )
            mine = slice(h * block, (h + 2) * block)
            product = wide(grads[t, mine, :]) * wide(saved)
            folded = product[:, :128]
            for k in range(128, LATENT, 128):
                folded = folded + product[:, k : k + 128]
            delta[t, :, mine] = jnp.sum(folded.T, axis=0, keepdims=True)

    @pl.when(step == 0)
    def _():
        for j in range(depth):
            for k in range(1, sides):
                side_key(k, j).wait_recv()
                core_key(k, j).start()
        for j in range(depth):
            for k in range(sides):
                core_key(k, j).wait_recv()

        def sort(p, carry):
            for k in range(SPAN):
                keys[p, k * block : (k + 1) * block, :] = gathered[
                    stored_ref[p * SPAN + k]
                ]
            return carry

        lax.fori_loop(0, tiles, sort, 0)

    to_side(0, step)

    late = table_ref[me, 6 * span]
    early = table_ref[me, 6 * span + 1]
    key_index = lax.broadcasted_iota(jnp.int32, (tile, rows), 0)
    row_index = lax.rem(lax.broadcasted_iota(jnp.int32, (tile, rows), 1), block)
    apart = key_index - row_index

    def visit(shared, i, carry):
        target = table_ref[me, i]
        query = queries[target]
        grad = grads[target]
        held = keys[table_ref[me, 2 * span + i]]
        scores = contract_last(held, query) * FACTOR
        visible = apart <= table_ref[me, 3 * span + i]
        weights = jnp.where(visible, jnp.exp(scores - logsum_ref[target]), 0.0)
        dprobs = contract_last(held[:, :LATENT], grad)
        dscore = (weights * (dprobs - delta[target]) * FACTOR).astype(jnp.bfloat16)
        rounded = weights.astype(jnp.bfloat16)
        from_keys = contract_first(dscore, held)
        if shared:
            upper = jnp.broadcast_to(table_ref[me, span + i], (rows, WIDE)) > 0
            query_sums[0] += jnp.where(upper, from_keys, 0.0)
            query_sums[1] += jnp.where(upper, 0.0, from_keys)
        else:
            query_sums[0] += from_keys
        from_scores = jnp.dot(dscore, query, preferred_element_type=jnp.float32)
        from_values = jnp.dot(rounded, grad, preferred_element_type=jnp.float32)
        mine = pl.ds(i * SPAN, SPAN)
        from_scores = from_scores.reshape(SPAN, block, WIDE)
        from_values = from_values.reshape(SPAN, block, LATENT)
        slots[mine, :, :LATENT] += from_scores[:, :, :LATENT] + from_values
        slots[mine, :, LATENT:] += from_scores[:, :, LATENT:]
        return carry

    lax.fori_loop(0, tiles // 2, functools.partial(visit, False), 0)
    lax.fori_loop(tiles // 2, tiles + 1, functools.partial(visit, True), 0)

    to_depth(0, step)

    @pl.when(step > 0)
    def _():
        to_depth(1, step - 1)

    for h in range(group):
        mine = slice(h * block, (h + 1) * block)
        cols = slice(h * NOPE_DIM, (h + 1) * NOPE_DIM)
        halves = [query_sums[late, mine, :], query_sums[early, mine, :]]
        grad_query = jnp.concatenate([x[:, :LATENT] for x in halves], axis=0)
        grad_query = grad_query.astype(jnp.bfloat16)
        d_nope_ref[:, cols] = jnp.dot(
            grad_query, key_up_ref[:, cols], preferred_element_type=jnp.float32
        ).astype(jnp.bfloat16)
        put_weight(1, h, contract_first(grad_query, nope_ref[:, cols]))
    start_weight(1, step)
    for t in range(2):
        held = slice(t * block, (t + 1) * block)
        source = late if t == 0 else early
        for h in range(0, group, 2):
            pair = [
                query_sums[source, k * block : (k + 1) * block, LATENT:][:, :ROPE_DIM]
                for k in (h, h + 1)
            ]
            d_rope_ref[held, h * ROPE_DIM : (h + 2) * ROPE_DIM] = jnp.concatenate(
                pair, axis=1
            ).astype(jnp.bfloat16)

    @pl.when(step == steps - 1)
    def _():
        def chosen(at):
            return jnp.broadcast_to(table_ref[me, at], (SPAN, block, WIDE)) > 0

        def combine(t, carry):
            here = pl.ds(t * SPAN, SPAN)
            there = pl.ds((tiles - 1 - t) * SPAN, SPAN)
            other = slots[there]
            above = chosen(4 * span + t)
            lowest = chosen(5 * span + t)
            slots[here] = (
                slots[here]
                + jnp.where(above, other, 0.0)
                + jnp.where(lowest, slots[tiles * SPAN :], 0.0)
            )
            slots[there] = jnp.where(above, 0.0, other)
            return carry

        lax.fori_loop(0, tiles // 2, combine, 0)

        for i in range(sides):

            def restore(j, carry):
                for c in range(2):
                    for half in range(2):
                        b = ((i * depth + j) * 2 + c) * 2 + half
                        k_part[i, j, c, half * block : (half + 1) * block, :] = slots[
                            order_ref[b]
                        ].astype(k_part.dtype)
                return carry

            lax.fori_loop(0, depth, restore, 0)

        def rows_of(target):
            return pl.ds(pl.multiple_of(target * share, share), share)

        pieces = WIDE // PIECE
        cols = [slice(c * PIECE, (c + 1) * PIECE) for c in range(pieces)]
        keys_core = [
            remote(
                k_part.at[:, :, 1 - core, :, cols[c]],
                k_recv1.at[c],
                "core",
                1 - core,
                both(k1, c),
            )
            for c in range(pieces)
        ]
        for copy in keys_core:
            copy.start()
        keys_head, keys_side, keys_depth = [], [], []
        for c in range(pieces):
            keys_core[c].wait_recv()
            for i in range(sides):
                for j in range(depth):
                    total = wide(k_part[i, j, core, :, cols[c]]) + wide(k_recv1[c, i, j])
                    k_recv1[c, i, j] = total.astype(k_recv1.dtype)
            copies = [
                remote(
                    k_recv1.at[c, :, :, rows_of(partner("head", k)), :],
                    k_recv2.at[c, k - 1],
                    "head",
                    partner("head", k),
                    both(k2, c, k - 1),
                )
                for k in range(1, heads)
            ]
            for copy in copies:
                copy.start()
            keys_head.append(copies)
        to_side(1, step)

        def head_to_side(c):
            for copy in keys_head[c]:
                copy.wait_recv()
            for i in range(sides):
                for j in range(depth):
                    total = wide(k_recv1[c, i, j, rows_of(head), :])
                    for k in range(heads - 1):
                        total = total + wide(k_recv2[c, k, i, j])
                    k_sum2[c, i, j] = total.astype(k_sum2.dtype)
            copies = [
                remote(
                    k_sum2.at[c, partner("inner", k)],
                    k_recv3.at[c, k - 1],
                    "inner",
                    partner("inner", k),
                    both(k3, c, k - 1),
                )
                for k in range(1, sides)
            ]
            for copy in copies:
                copy.start()
            keys_side.append(copies)

        def side_to_depth(c):
            for copy in keys_side[c]:
                copy.wait_recv()
            for j in range(depth):
                total = wide(k_sum2[c, inner, j])
                for k in range(sides - 1):
                    total = total + wide(k_recv3[c, k, j])
                k_sum3[c, j] = total.astype(k_sum3.dtype)
            copies = [
                remote(
                    k_sum3.at[c, partner("depth", k)],
                    k_recv4.at[c, k - 1],
                    "depth",
                    partner("depth", k),
                    both(k4, c, k - 1),
                )
                for k in range(1, depth)
            ]
            for copy in copies:
                copy.start()
            keys_depth.append(copies)

        for c in range(pieces):
            head_to_side(c)
            if c == 1:
                to_depth(1, step)
            if c > 0:
                side_to_depth(c - 1)
        side_to_depth(pieces - 1)

        def finish(g, carry):
            finish_weight(0, g, d_value_up_ref)
            finish_weight(1, g, d_key_up_ref)
            return carry

        lax.fori_loop(0, steps, finish, 0)
        for c in range(pieces):
            for copy in keys_depth[c]:
                copy.wait_recv()
            total = wide(k_sum3[c, level])
            for k in range(depth - 1):
                total = total + wide(k_recv4[c, k])
            k_own[rows_of(head), cols[c]] = total.astype(k_own.dtype)
        keys_last = [
            remote(
                k_own.at[rows_of(head), :],
                k_own.at[rows_of(head), :],
                "head",
                partner("head", k),
                both(k5, k - 1),
            )
            for k in range(1, heads)
        ]
        for copy in keys_last:
            copy.start()

        def drain(g, carry):
            finish_sends(0, g)
            finish_sends(1, g)
            return carry

        lax.fori_loop(0, steps, drain, 0)
        for k in range(1, depth):
            depth_key(k).wait_send()
        for j in range(depth):
            for k in range(1, sides):
                side_key(k, j).wait_send()
            for k in range(sides):
                core_key(k, j).wait_send()
        for copy in keys_core + sum(keys_head + keys_side + keys_depth, []):
            copy.wait_send()
        for copy in keys_last:
            copy.wait()
        d_latent_ref[...] = k_own[:, :LATENT]
        d_key_rope_ref[...] = k_own[:, LATENT:][:, :ROPE_DIM]


def fused(
    sizes,
    group,
    stored,
    order,
    table,
    latent,
    key_rope,
    query_nope,
    query_rope,
    key_up,
    value_up,
    saved,
    upstream,
    logsum,
):
    depth, sides, heads = sizes["depth"], sizes["inner"], sizes["head"]
    owners = sides * depth * 2
    tokens = query_nope.shape[0]
    local_heads = query_nope.shape[1] // NOPE_DIM
    steps = local_heads // group
    block = tokens // 2
    length = owners * tokens
    blocks = length // block
    rows = group * block
    share = LATENT // owners
    totals = logsum.reshape(2, block, local_heads).transpose(0, 2, 1)
    totals = totals.reshape(2, 1, local_heads * block)
    whole = lambda i: (0, 0)
    part = lambda i: (0, i)
    narrow = lambda *shape: pltpu.VMEM(shape, jnp.bfloat16)
    full = lambda *shape: pltpu.VMEM(shape, jnp.float32)
    dma = lambda *shape: pltpu.SemaphoreType.DMA(shape)
    piece = (share, group * NOPE_DIM)
    mine = (tokens, WIDE)
    split = (tokens // heads, PIECE)
    pieces = WIDE // PIECE
    pairs = length * local_heads * tokens // 2
    results = pl.pallas_call(
        functools.partial(fused_kernel, sizes, group, block, blocks),
        grid=(steps,),
        in_specs=[
            pl.BlockSpec(memory_space=pltpu.SMEM),
            pl.BlockSpec(memory_space=pltpu.SMEM),
            pl.BlockSpec(memory_space=pltpu.SMEM),
            pl.BlockSpec((tokens, LATENT), whole),
            pl.BlockSpec((tokens, ROPE_DIM), whole),
            pl.BlockSpec((tokens, group * NOPE_DIM), part),
            pl.BlockSpec((tokens, group * ROPE_DIM), part),
            pl.BlockSpec((LATENT, group * NOPE_DIM), part),
            pl.BlockSpec((LATENT, group * VALUE_DIM), part),
            pl.BlockSpec((tokens, group * LATENT), part),
            pl.BlockSpec((tokens, group * VALUE_DIM), part),
            pl.BlockSpec((2, 1, rows), lambda i: (0, 0, i)),
        ],
        out_specs=[
            pl.BlockSpec((tokens, group * NOPE_DIM), part),
            pl.BlockSpec((tokens, group * ROPE_DIM), part),
            pl.BlockSpec((tokens, LATENT), whole),
            pl.BlockSpec((tokens, ROPE_DIM), whole),
            pl.BlockSpec((share, local_heads * NOPE_DIM), whole),
            pl.BlockSpec((share, local_heads * VALUE_DIM), whole),
        ],
        scratch_shapes=[
            narrow(blocks, block, WIDE),
            narrow(blocks // SPAN, SPAN * block, WIDE),
            full(blocks + SPAN, block, WIDE),
            narrow(2, rows, WIDE),
            narrow(2, rows, LATENT),
            full(2, 1, rows),
            full(2, rows, WIDE),
            narrow(2, steps, sides, depth, 2, *piece),
            narrow(2, steps, sides, depth, *piece),
            narrow(2, steps, sides - 1, depth, *piece),
            narrow(2, steps, depth, *piece),
            narrow(2, steps, depth - 1, *piece),
            narrow(sides, depth, 2, *mine),
            narrow(pieces, sides, depth, tokens, PIECE),
            narrow(pieces, heads - 1, sides, depth, *split),
            narrow(pieces, sides, depth, *split),
            narrow(pieces, sides - 1, depth, *split),
            narrow(pieces, depth, *split),
            narrow(pieces, depth - 1, *split),
            narrow(*mine),
            dma(2, depth - 1),
            dma(2, sides - 1, depth),
            dma(2, sides, depth),
            dma(2, 2, steps),
            dma(2, 2, steps, sides - 1),
            dma(2, 2, steps, depth - 1),
            dma(2, pieces),
            dma(2, pieces, heads - 1),
            dma(2, pieces, sides - 1),
            dma(2, pieces, depth - 1),
            dma(2, heads - 1),
        ],
        out_shape=[
            jax.ShapeDtypeStruct(query_nope.shape, jnp.bfloat16),
            jax.ShapeDtypeStruct(query_rope.shape, jnp.bfloat16),
            jax.ShapeDtypeStruct((tokens, LATENT), jnp.bfloat16),
            jax.ShapeDtypeStruct((tokens, ROPE_DIM), jnp.bfloat16),
            jax.ShapeDtypeStruct((share, local_heads * NOPE_DIM), jnp.float32),
            jax.ShapeDtypeStruct((share, local_heads * VALUE_DIM), jnp.float32),
        ],
        compiler_params=pltpu.CompilerParams(
            collective_id=0, has_side_effects=True, vmem_limit_bytes=VMEM
        ),
        cost_estimate=pl.CostEstimate(
            flops=pairs * 2 * 2752, bytes_accessed=20 * 1024 * 1024, transcendentals=pairs
        ),
        name="latent_attention_backward",
    )(
        stored,
        order,
        table,
        latent,
        key_rope,
        query_nope,
        query_rope,
        key_up,
        value_up,
        saved,
        upstream,
        totals,
    )
    return hand_over(results)


def hand_over_kernel(count, *refs):
    for i in range(count):
        refs[count + i][...] = refs[i][...]


def hand_over(arrays):
    count = len(arrays)
    return pl.pallas_call(
        functools.partial(hand_over_kernel, count),
        in_specs=[pl.BlockSpec(memory_space=pltpu.VMEM)] * count,
        out_specs=[pl.BlockSpec(memory_space=pltpu.VMEM)] * count,
        out_shape=[jax.ShapeDtypeStruct(x.shape, x.dtype) for x in arrays],
        compiler_params=pltpu.CompilerParams(vmem_limit_bytes=VMEM),
        name="hand_over",
    )(*arrays)


def local(
    query_nope,
    query_rope,
    latent,
    key_rope,
    key_up,
    value_up,
    latent_out,
    out_grad,
    logsum,
    block_order,
):
    axes = ("inner", "outer")
    heads = query_nope.shape[1] // NOPE_DIM
    blocks = block_order.shape[0]
    group = min(8, heads)
    sizes = {
        "head": lax.axis_size("head"),
        "inner": lax.axis_size("inner"),
        "depth": lax.axis_size("outer") // 2,
        "core": 2,
    }
    index = lax.iota(jnp.int32, blocks)
    held = (block_order[:, None] == index[None, :]).astype(jnp.int32)
    stored = jnp.sum(held * index[:, None], axis=0)
    tiles = blocks // SPAN
    span = tiles + 1
    pair = block_order.reshape(-1, 2)
    first, second = pair[:, :1], pair[:, 1:]
    late = (second > first).astype(jnp.int32)
    later, earlier = jnp.maximum(first, second), jnp.minimum(first, second)
    top, low = later // SPAN, earlier // SPAN
    column = np.arange(FIELDS * span, dtype=np.int32)[None, :]
    field, slot = column // span, column % span
    upper = slot <= jnp.minimum(top, tiles - 1)
    tile_of = jnp.where(upper, slot, jnp.where(slot == tiles, low, tiles - 1 - slot))
    limit = (jnp.where(upper, later, earlier) - tile_of * SPAN) * (query_nope.shape[0] // 2)
    above = (tiles - 1 - slot > top).astype(jnp.int32)
    table = jnp.where(slot == 0, late, 1 - late)
    table = jnp.where(field == 5, (slot == low).astype(jnp.int32), table)
    table = jnp.where(field == 4, above, table)
    table = jnp.where(field == 3, limit, table)
    table = jnp.where(field == 2, tile_of, table)
    table = jnp.where(field == 1, upper.astype(jnp.int32), table)
    table = jnp.where(field == 0, jnp.where(upper, late, 1 - late), table)
    return fused(
        sizes,
        group,
        stored,
        block_order,
        table,
        latent,
        key_rope,
        query_nope,
        query_rope,
        key_up,
        value_up,
        latent_out,
        out_grad,
        logsum,
    )


def solution(mesh):
    placed = (
        P(("inner", "outer"), "head"),
        P(("inner", "outer"), "head"),
        P(("inner", "outer"), None),
        P(("inner", "outer"), None),
        P(None, "head"),
        P(None, "head"),
        P(("inner", "outer"), "head"),
        P(("inner", "outer"), "head"),
        P(("inner", "outer"), "head"),
        P(),
    )
    return jax.shard_map(
        local,
        mesh=mesh,
        in_specs=placed,
        out_specs=(
            P(("inner", "outer"), "head"),
            P(("inner", "outer"), "head"),
            P(("inner", "outer"), None),
            P(("inner", "outer"), None),
            P(("inner", "outer"), "head"),
            P(("inner", "outer"), "head"),
        ),
        check_vma=False,
    )
```
